256 devices in a mesh: row: 16 (over x, y), col: 16 (over z, core).
Axes of the slice: x: 4, y: 4, z: 8, core: 2. Of those that a mesh axis runs over, the one named last changes fastest.
Arguments:
- hidden_rows: bfloat16 [8192, 4096], P('row', 'col'), may hold values from -64 to 64
- code_table: bfloat16 [131072, 4096], P('row', 'col'), may hold values from -6 to 6
- labels: int32 [8192], P('row'), may hold values from 0 to 131071, as said below
- targets: int32 [8192], P('row'), may hold values from 0 to 8191
- sub_codebook: bfloat16 [4096, 8192], P('row', 'col'), may hold values from -1 to 1
Outputs:
- row_loss: float32 [8192], P('row')
- grad_hidden: bfloat16 [8192, 4096], P('row', 'col')
- grad_codes: bfloat16 [131072, 4096], P('row', 'col')
- grad_sub: bfloat16 [4096, 8192], P('row', 'col')
The draws below stay inside these ranges and needn't reach their ends.
Inputs may be any that keep to these rules, and one draw needn't show every extreme that they name: Within each aligned block of 512 rows, at most 64 labels fall into any one aligned range of 8192 codes, and exactly 64 fall into some range.
All inputs are finite; a program needn't handle non-finite values.
Results may differ from the reference program's by a relative error of at most 0.022.
Values may be sent and summed in bfloat16 or wider, within the bound.
A program may use at most 128 MiB of HBM per device.

```python
import jax
import jax.numpy as jnp
from jax import lax

D = 4096
V2 = 8192
ROW_DEV = 512
ROWS = 8192
V1 = 131072
CAP = 64
N_ROW = 16
N_COL = 16


def shared_codebook(key):
    return jnp.clip(jax.random.normal(key, (D, V2), jnp.float32), -6.0, 6.0) * D ** (-0.5)


def draw_sub_codebook(key, part):
    return shared_codebook(key).astype(jnp.bfloat16)


def draw_hidden_rows(key, part):
    key = jax.random.fold_in(key, 2)
    keys = jax.random.split(key, 1)
    result = jax.random.normal(keys[0], (ROWS, D), jnp.float32)
    return jnp.clip(result, -64.0, 64.0).astype(jnp.bfloat16)


def draw_labels(key, part):
    key = jax.random.fold_in(key, 5)
    groups = N_ROW
    share = V1 // N_ROW
    blocks = ROWS // ROW_DEV

    def one_block(block_key):
        keys = jax.random.split(block_key, 4)
        crowded = jax.random.randint(keys[0], (), 0, groups)
        spread = jax.random.permutation(keys[1], (groups - 1) * CAP)[:ROW_DEV - CAP] // CAP
        spread = jnp.where(spread >= crowded, spread + 1, spread).astype(jnp.int32)
        owners = jnp.concatenate([jnp.full((CAP,), crowded, jnp.int32), spread])
        owners = jax.random.permutation(keys[2], owners)
        offsets = jax.random.randint(keys[3], (ROW_DEV,), 0, share)
        return (owners * share + offsets).astype(jnp.int32)
    return jax.vmap(one_block)(jax.random.split(key, blocks)).reshape(ROWS).astype(jnp.int32)


def with_ends(drawn, key, low, top_value):
    extent = drawn.shape
    index_at = [jax.random.randint(jax.random.fold_in(key, axis), (), 0, extent[axis]) for axis in range(len(extent))]
    drawn = drawn.at[tuple(index_at)].set(low)
    longest = extent.index(max(extent))
    index_at[longest] = (index_at[longest] + 1) % extent[longest]
    return drawn.at[tuple(index_at)].set(top_value)


def steps_of(own_key, shape, cuts, least, top_value):
    gain, own = 1.0, jax.random.fold_in(own_key, 6)
    for dim, shards_of in cuts:
        steps = jnp.exp(jax.random.uniform(jax.random.fold_in(own, dim), (shards_of,), jnp.float32, least / len(cuts), top_value / len(cuts)))
        gain = gain * jnp.repeat(steps, shape[dim] // shards_of).reshape([-1 if axis == dim else 1 for axis in range(len(shape))])
    return gain


def bell_draw(stream_key, shape, width, bound, pieces=(), held_as=jnp.bfloat16):
    values = jax.random.normal(stream_key, shape, jnp.float32) * width
    if len(pieces) > 0:
        values = steps_of(stream_key, shape, pieces, -0.22, 0.18) * values
    return jnp.clip(values, min=-bound, max=bound).astype(held_as)


def setup_inputs(seed: int = 0) -> dict:
    key_list = jax.random.split(jax.random.key(seed), 6)
    return {
        "hidden_rows": draw_hidden_rows(jax.random.fold_in(key_list[5], 71), 0),
        "code_table": bell_draw(key_list[1], (V1, D), 1.0, 6.0, ((0, 16), (1, 16))),
        "labels": draw_labels(jax.random.fold_in(key_list[5], 71), 0),
        "targets": with_ends(jax.random.randint(key_list[3], (ROWS,), 0, V2), jax.random.fold_in(key_list[3], 1), 0, V2 - 1).astype(jnp.int32),
        "sub_codebook": draw_sub_codebook(jax.random.fold_in(key_list[5], 71), 0),
    }


def reference(hidden_rows, code_table, labels, targets, sub_codebook):
    code_rows = code_table[labels]
    query_rows = (hidden_rows.astype(jnp.float32) + code_rows.astype(jnp.float32)).astype(jnp.bfloat16)
    logits = jnp.dot(query_rows, sub_codebook, preferred_element_type=jnp.float32)
    row_peak = jnp.max(logits, axis=1)
    exp_total = jnp.sum(jnp.exp(logits - row_peak[:, None]), axis=1)
    log_total = row_peak + jnp.log(exp_total)
    target_logit = jnp.take_along_axis(logits, targets[:, None].astype(jnp.int32), axis=1)[:, 0]
    row_loss = log_total - target_logit
    onehot = (jnp.arange(V2, dtype=jnp.int32)[None, :] == targets[:, None]).astype(jnp.float32)
    dlogits = (jnp.exp(logits - log_total[:, None]) - onehot).astype(jnp.bfloat16)
    local_width = V2 // N_COL

    def block_term(carry, index):
        start = (index * local_width).astype(jnp.int32)
        block_grad = lax.dynamic_slice_in_dim(dlogits, start, local_width, 1)
        block_codes = lax.dynamic_slice_in_dim(sub_codebook, start, local_width, 1)
        partial_grad = lax.dot_general(block_grad, block_codes, (((1,), (1,)), ((), ())), preferred_element_type=jnp.float32)
        rounded = lax.optimization_barrier(partial_grad.astype(jnp.bfloat16))
        return carry + rounded.astype(jnp.float32), None

    grad_query, unused = lax.scan(block_term, jnp.zeros((ROWS, D), jnp.float32), jnp.arange(N_COL, dtype=jnp.int32))
    grad_hidden = grad_query.astype(jnp.bfloat16)
    grad_codes = jax.ops.segment_sum(grad_query, labels, num_segments=V1).astype(jnp.bfloat16)
    grad_sub = jnp.dot(query_rows.T, dlogits, preferred_element_type=jnp.float32).astype(jnp.bfloat16)
    return (row_loss, grad_hidden, grad_codes, grad_sub)
```

```python
import jax
import jax.numpy as jnp
from jax import lax
from jax.experimental import pallas as pl
from jax.experimental.pallas import tpu as pltpu
from jax.sharding import PartitionSpec as P

MESH = pl.DeviceIdType.MESH
F32, BF16, I32 = jnp.float32, jnp.bfloat16, jnp.int32

NX, NY, NZ = 4, 4, 8
NR, NC = NX * NY, 2 * NZ
ROWS, FEAT, CODES = 512, 256, 512
HALF = 256
TABLE = 8192
CAP = 64
CHUNK = 1024
NT = (((1,), (1,)), ((), ()))


class Ids:
    def __init__(self):
        self.at = {}
        for name in ("want", "serve", "stat", "ret"):
            for rel in range(16):
                self((name, rel))
        for half in range(2):
            for j in range(5):
                for part in range(4):
                    self(("w", half, j, part))
                    self(("x", half, j, part))
        for way in (1, -1):
            for s in range(4):
                for h in range(2):
                    self(("q", way, s + 1, h))
                    self(("z", way, s, h))
        for dz in range(NZ):
            self(("gs", dz))
            for h in range(2):
                self(("qs", dz, h))

    def __call__(self, name):
        return self.at.setdefault(name, len(self.at))


IDS = Ids()
N_IDS = len(IDS.at)


def dot(a, b, dims=(((1,), (0,)), ((), ()))):
    return lax.dot_general(a, b, dims, preferred_element_type=F32)


def main_kernel(
    hid, table, lab, tgt, wsub,
    loss_o, gh_o, gs_o, ret_o, ask_o,
    wf, qf, tb, tf, wbuf, askv, asks, srv32, srv, fet, pm, mm, lg, dl, dlt,
    stat_s, stat_r, gqo, gqs, sibr, zr, gt, xq, xl, outb,
    lsem, ssem, rsem,
):
    row = lax.axis_index("row")
    col = lax.axis_index("col")
    x, y = row // NY, row % NY
    z, k = col // 2, col % 2

    def rdev(r):
        return (r, col)

    def cdev(c):
        return (row, c)

    def xn(d):
        return rdev(((x + d + NX) % NX) * NY + y)

    def yn(d):
        return rdev(x * NY + (y + d + NY) % NY)

    def zn(d):
        return cdev(((z + d + NZ) % NZ) * 2 + k)

    sib = cdev(z * 2 + 1 - k)

    def slot(dx, dy):
        return ((x + dx) % NX) * NY + (y + dy) % NY

    def cp(i, src, dst, dev):
        return pltpu.make_async_remote_copy(
            src_ref=src, dst_ref=dst, send_sem=ssem.at[i], recv_sem=rsem.at[i],
            device_id=dev, device_id_type=MESH,
        )

    sent = []

    def send(name, src, dst, dev):
        c = cp(IDS(name), src, dst, dev)
        c.start()
        sent.append(c)

    def recv(name, dst):
        cp(IDS(name), dst, dst, sib).wait_recv()

    own_w = pltpu.make_async_copy(wsub, wf.at[row], lsem.at[0])
    own_w.start()

    def table_copy(i):
        return pltpu.make_async_copy(
            table.at[pl.ds(i * CHUNK, CHUNK), :], tb.at[i % 2], lsem.at[2 + i % 2]
        )

    table_copy(0).start()
    table_copy(1).start()

    barrier = pltpu.get_barrier_semaphore()
    for rel in range(1, 16):
        pl.semaphore_signal(barrier, inc=1, device_id=rdev((row + rel) % NR), device_id_type=MESH)
        pl.semaphore_signal(barrier, inc=1, device_id=cdev((col + rel) % NC), device_id_type=MESH)

    lab_row = jnp.concatenate([lab[i:i + 1, :] for i in range(4)], axis=1)
    owner = lax.shift_right_logical(lab_row, 13)
    off = lab_row & (TABLE - 1)
    member = (owner == lax.broadcasted_iota(I32, (NR, ROWS), 0)).astype(F32)
    before = (
        lax.broadcasted_iota(I32, (ROWS, ROWS), 0) < lax.broadcasted_iota(I32, (ROWS, ROWS), 1)
    ).astype(F32).astype(BF16)
    rank = jnp.sum(member * dot(member.astype(BF16), before), axis=0, keepdims=True)
    rank = rank.astype(I32)
    at_rank = (rank == lax.broadcasted_iota(I32, (128, ROWS), 0)).astype(F32).astype(BF16)
    hi = lax.shift_right_logical(off, 7).astype(F32)
    lo = (off & 127).astype(F32)
    both = jnp.concatenate([member * hi, member * lo], axis=0).astype(BF16)
    spread = dot(both, at_rank, NT)
    wanted = (spread[:NR] * 128.0 + spread[NR:]).astype(I32)
    for g in range(NR):
        wbuf[g] = jnp.broadcast_to(wanted[g:g + 1, :], (8, 128))
    place = owner * CAP + rank

    pl.semaphore_wait(barrier, 30)
    for rel in range(1, NR):
        to = (row + rel) % NR
        send(("want", rel), wbuf.at[to], askv.at[row], rdev(to))
    own_w.wait()

    def whalf(s, half, a=0, n=128):
        return wf.at[s, pl.ds(half * 128 + a, n), :]

    def wring(half, j):
        if j == 4:
            return (xn, lambda d: slot(d, 0)) if half == 0 else (yn, lambda d: slot(0, d))
        if half == 0:
            return yn, lambda d: slot(j, d)
        return xn, lambda d: slot(d, j)

    def w_own(half, j):
        nb, at = wring(half, j)
        send(("w", half, j, 0), whalf(at(0), half), whalf(at(0), half), nb(1))
        send(("w", half, j, 1), whalf(at(0), half), whalf(at(0), half), nb(-1))

    def w_mid(half, j, side):
        nb, at = wring(half, j)
        s = at(3) if side == 0 else at(1)
        recv(("w", half, j, side), whalf(s, half))
        part = whalf(s, half, 64 * side, 64)
        send(("w", half, j, 2 + side), part, part, nb(1 - 2 * side))

    def w_last(half, j):
        nb, at = wring(half, j)
        for side in range(2):
            recv(("w", half, j, 2 + side), whalf(at(2), half, 64 * side, 64))

    for half in range(2):
        w_own(half, 4)
    for half in range(2):
        w_own(half, 0)

    for i in range(TABLE // CHUNK):
        table_copy(i).wait()

        @pl.loop(0, CHUNK // 128)
        def _(t, i=i):
            tf[pl.ds(i * CHUNK + t * 128, 128), :] = tb[i % 2, pl.ds(t * 128, 128), :].astype(F32)

        if i + 2 < TABLE // CHUNK:
            table_copy(i + 2).start()

    askv[row] = wbuf[row]
    for rel in range(1, NR):
        recv(("want", rel), askv.at[(row - rel + NR) % NR])
    for r in range(NR):
        ask_o[r:r + 1, :] = askv[r, 0:1, :]
    to_smem = pltpu.make_async_copy(ask_o, asks, lsem.at[1])
    to_smem.start()
    to_smem.wait()

    def gather(r):
        @pl.loop(0, CAP // 8)
        def _(t):
            for u in range(8):
                i = asks[r, t * 8 + u] & (TABLE - 1)
                srv32[pl.ds(t * 8 + u, 1), :] = tf[pl.ds(i, 1), :]

    @pl.loop(1, NR)
    def _(rel):
        to = (row + rel) % NR
        gather(to)
        srv[to] = srv32[...].astype(BF16)
        cp(IDS(("serve", 0)) + rel, srv.at[to], fet.at[row], rdev(to)).start()

    gather(row)
    fet[row] = srv32[...].astype(BF16)

    place_f = place.astype(F32)
    for i in range(4):
        wide = jnp.broadcast_to(place_f[:, i * 128:(i + 1) * 128], (128, 128)).T.astype(I32)
        for t in range(8):
            pm[i * 128:(i + 1) * 128, t * 128:(t + 1) * 128] = (
                wide == lax.broadcasted_iota(I32, (128, 128), 1) + t * 128
            ).astype(F32).astype(BF16)
    for t in range(8):
        mm[t * 128:(t + 1) * 128, :] = (
            place == lax.broadcasted_iota(I32, (128, ROWS), 0) + t * 128
        ).astype(F32).astype(BF16)

    for half in range(2):
        for side in range(2):
            w_mid(half, 4, side)
            w_own(half, 3 - 2 * side)

    for rel in range(1, NR):
        recv(("serve", rel), fet.at[(row - rel + NR) % NR])

    def qpart(s, h):
        return qf.at[s, pl.ds(h * HALF, HALF), :]

    for h in range(2):
        rows = pl.ds(h * HALF, HALF)
        code = dot(pm[rows, :], fet[...].reshape(NR * CAP, FEAT))
        qf[col, rows, :] = (hid[rows, :].astype(F32) + code).astype(BF16)
        for way in (1, -1):
            send(("q", way, 1, h), qpart(col, h), qpart(col, h), zn(way))
        send(("qs", 0, h), qpart(col, h), qpart(col, h), sib)

    def q_step(s):
        for h in range(2):
            for way in (1, -1):
                if s == 4 and (way == 1) != (h == 0):
                    continue
                at = ((z - way * s + NZ) % NZ) * 2 + k
                piece = qpart(at, h)
                recv(("q", way, s, h), piece)
                if s < 3 or (s == 3 and (way == 1) == (h == 0)):
                    send(("q", way, s + 1, h), piece, piece, zn(way))
                send(("qs", (-way * s) % NZ, h), piece, piece, sib)

    def logits_of(n_ways, s):
        for dz in ([s, NZ - s] if 0 < s < 4 else [s]):
            for h in range(2):
                recv(("qs", dz, h), qpart(((z + dz) % NZ) * 2 + 1 - k, h))

        @pl.loop(0, 2 * n_ways)
        def _(t):
            dz = jnp.where(t % n_ways == 0, s, NZ - s)
            core = t // n_ways
            at = ((z + dz) % NZ) * 2 + core
            for h in range(2):
                rows = pl.ds(h * HALF, HALF)
                lg[rows, :] += dot(qf[at, rows, :], wf[at])

    for half in range(2):
        for side in range(2):
            w_mid(half, 0, side)
    for half in range(2):
        w_last(half, 4)
        w_own(half, 2)
    q_step(1)
    for j in (3, 1):
        for half in range(2):
            for side in range(2):
                w_mid(half, j, side)
    q_step(2)
    for half in range(2):
        for side in range(2):
            w_mid(half, 2, side)
    for j in (0, 3, 1, 2):
        for half in range(2):
            w_last(half, j)
    lg[...] = jnp.zeros((ROWS, CODES), F32)
    logits_of(1, 0)
    q_step(3)
    logits_of(2, 1)
    logits_of(2, 2)
    q_step(4)
    logits_of(2, 3)
    logits_of(1, 4)

    lane = lax.broadcasted_iota(I32, (128, 128), 1)

    def hit_of(i, j):
        wide = jnp.broadcast_to(tgt[i:i + 1, :].astype(F32), (128, 128)).T.astype(I32)
        return wide - col * CODES == lane + j * 128

    for i in range(4):
        rows = slice(i * 128, (i + 1) * 128)
        v = lg[rows, :]
        peak = jnp.max(v, axis=1, keepdims=True)
        log_sum = peak + jnp.log(jnp.sum(jnp.exp(v - peak), axis=1, keepdims=True))
        hits = jnp.concatenate([hit_of(i, j) for j in range(4)], axis=1)
        target = jnp.sum(jnp.where(hits, v, 0.0), axis=1, keepdims=True)
        pair = jnp.where(lane == 0, log_sum, jnp.where(lane == 1, target, 0.0)).T
        stat_s[i:i + 1, :] = pair[0:1, :]
        stat_s[4 + i:5 + i, :] = pair[1:2, :]
    stat_r[col] = stat_s[...]
    for rel in range(1, NC):
        send(("stat", rel), stat_s, stat_r.at[col], cdev((col + rel) % NC))
    for rel in range(1, NC):
        recv(("stat", rel), stat_r.at[(col - rel + NC) % NC])
    logs = stat_r[:, 0:4, :]
    top = jnp.max(logs, axis=0)
    log_total = top + jnp.log(jnp.sum(jnp.exp(logs - top[None]), axis=0))
    loss_o[...] = log_total - jnp.sum(stat_r[:, 4:8, :], axis=0)
    for i in range(4):
        wide = jnp.broadcast_to(log_total[i:i + 1, :], (128, 128)).T
        for j in range(4):
            v = lg[i * 128:(i + 1) * 128, j * 128:(j + 1) * 128]
            d = jnp.exp(v - wide) - hit_of(i, j).astype(F32)
            dl[i * 128:(i + 1) * 128, j * 128:(j + 1) * 128] = d.astype(BF16)
            dlt[j * 128:(j + 1) * 128, i * 128:(i + 1) * 128] = d.T.astype(BF16)

    def grad_block(dz):
        at = ((z + dz) % NZ) * 2
        gqs[dz] = dot(dl[...], wf[at + 1 - k], NT).astype(BF16)
        send(("gs", dz), gqs.at[dz], sibr.at[dz], sib)
        gqo[dz] = dot(dl[...], wf[at + k], NT).astype(BF16)

    def pair_up(dz):
        recv(("gs", dz), sibr.at[dz])
        gqo[dz] = (gqo[dz].astype(F32) + sibr[dz].astype(F32)).astype(BF16)

    def sub_block(dx, dy):
        s = slot(dx, dy)
        gt[s] = dot(dlt[...], qf[s]).astype(BF16)

    def zpart(dz, h):
        return gqo.at[dz % NZ, pl.ds(h * HALF, HALF), :]

    def zsend(way, d, h):
        send(("z", way, d, h), zpart(way * (d + 1), h), zr.at[(1 - way) // 2, d, h], zn(way))

    def zadd(way, d, h):
        got = zr.at[(1 - way) // 2, d, h]
        recv(("z", way, d, h), got)
        part = zpart(way * d, h)
        part[...] = (part[...].astype(F32) + got[...].astype(F32)).astype(BF16)

    def xring(half, j):
        if j == 4:
            return (xn, lambda d: slot(d, 0)) if half == 0 else (yn, lambda d: slot(0, d))
        if half == 0:
            return yn, lambda d: slot(j, d)
        return xn, lambda d: slot(d, j)

    def xpart(s, half, a=0, n=256):
        return gt.at[s, pl.ds(half * 256 + a, n), :]

    def x_start(half, j):
        nb, at = xring(half, j)
        for side in range(2):
            send(("x", half, j, side), xpart(at(2), half, 128 * side, 128), xq.at[half, j, side], nb(1 - 2 * side))

    def x_mid(half, j):
        nb, at = xring(half, j)
        for side in range(2):
            got = xq.at[half, j, side]
            recv(("x", half, j, side), got)
            s = at(1) if side == 0 else at(3)
            part = xpart(s, half, 128 * side, 128)
            part[...] = (part[...].astype(F32) + got[...].astype(F32)).astype(BF16)
            send(("x", half, j, 2 + side), xpart(s, half), xl.at[half, j, side], nb(1 - 2 * side))

    def x_end(half, j):
        nb, at = xring(half, j)
        for side in range(2):
            recv(("x", half, j, 2 + side), xl.at[half, j, side])
        part = xpart(at(0), half)
        part[...] = (
            part[...].astype(F32) + xl[half, j, 0].astype(F32) + xl[half, j, 1].astype(F32)
        ).astype(BF16)

    grad_block(4)
    grad_block(3)
    grad_block(5)
    sub_block(2, 2)
    pair_up(4)
    zsend(1, 3, 0)
    zsend(-1, 3, 1)
    for half in range(2):
        x_start(half, 2)
    pair_up(3)
    pair_up(5)
    zsend(1, 2, 1)
    zsend(-1, 2, 0)
    for d in (1, 3, 0):
        sub_block(2, d)
        sub_block(d, 2)
        for half in range(2):
            x_start(half, d)
    grad_block(2)
    grad_block(6)
    for half in range(2):
        x_mid(half, 2)
    pair_up(2)
    pair_up(6)
    for way, h in ((1, 0), (-1, 1)):
        zadd(way, 3, h)
        zsend(way, 2, h)
    sub_block(1, 1)
    sub_block(3, 1)
    sub_block(1, 3)
    sub_block(3, 3)
    sub_block(1, 0)
    sub_block(0, 1)
    sub_block(3, 0)
    sub_block(0, 3)
    sub_block(0, 0)
    for j in (1, 3):
        for half in range(2):
            x_mid(half, j)
    for way, h in ((1, 1), (-1, 0)):
        zadd(way, 2, h)
        zsend(way, 1, h)
    grad_block(1)
    grad_block(7)
    grad_block(0)
    for half in range(2):
        x_end(half, 2)
        x_start(half, 4)
    for half in range(2):
        x_mid(half, 0)
    pair_up(1)
    pair_up(7)
    for way, h in ((1, 0), (-1, 1)):
        zadd(way, 2, h)
        zsend(way, 1, h)
    for way, h in ((1, 1), (-1, 0)):
        zadd(way, 1, h)
        zsend(way, 0, h)
    for half in range(2):
        x_end(half, 1)
        x_end(half, 3)
    for half in range(2):
        x_mid(half, 4)
    for way, h in ((1, 0), (-1, 1)):
        zadd(way, 1, h)
        zsend(way, 0, h)
    pair_up(0)
    for half in range(2):
        x_end(half, 0)

    for way in (1, -1):
        for h in range(2):
            recv(("z", way, 0, h), zr.at[(1 - way) // 2, 0, h])
    for h in range(2):
        rows = pl.ds(h * HALF, HALF)
        total = gqo[0, rows, :].astype(F32) + zr[0, 0, h].astype(F32) + zr[1, 0, h].astype(F32)
        gh_o[rows, :] = total.astype(BF16)
    for t in range(8):
        moved = dot(mm[t * 128:(t + 1) * 128, :], gh_o[...]).astype(BF16)
        outb[2 * t] = moved[:CAP]
        outb[2 * t + 1] = moved[CAP:]
    for rel in range(1, NR):
        to = (row + rel) % NR
        send(("ret", rel), outb.at[to], ret_o.at[row], rdev(to))
    ret_o[row] = outb[row]
    for half in range(2):
        x_end(half, 4)
    gs_o[...] = gt[row].astype(F32).T.astype(BF16)
    for rel in range(1, NR):
        recv(("ret", rel), ret_o.at[(row - rel + NR) % NR])

    for c in sent:
        c.wait_send()

    @pl.loop(1, NR)
    def _(rel):
        cp(IDS(("serve", 0)) + rel, srv.at[0], fet.at[0], sib).wait_send()


def scatter_kernel(ret, ask, out):
    base = pl.program_id(0) * 256
    hits = (ask[...] - base == lax.broadcasted_iota(I32, (256, NR * CAP), 0)).astype(F32).astype(BF16)
    out[...] = dot(hits, ret[...]).astype(BF16)


def per_device(hidden_rows, code_table, labels, targets, sub_codebook):
    vmem = pl.BlockSpec(memory_space=pltpu.VMEM)
    loss, grad_hidden, grad_sub, returned, asked = pl.pallas_call(
        main_kernel,
        out_shape=(
            jax.ShapeDtypeStruct((4, 128), F32),
            jax.ShapeDtypeStruct((ROWS, FEAT), BF16),
            jax.ShapeDtypeStruct((FEAT, CODES), BF16),
            jax.ShapeDtypeStruct((NR, CAP, FEAT), BF16),
            jax.ShapeDtypeStruct((NR, 128), I32),
        ),
        in_specs=[vmem, pl.BlockSpec(memory_space=pl.ANY), vmem, vmem, vmem],
        out_specs=[vmem] * 5,
        scratch_shapes=[
            pltpu.VMEM((NR, FEAT, CODES), BF16),
            pltpu.VMEM((NC, ROWS, FEAT), BF16),
            pltpu.VMEM((2, CHUNK, FEAT), BF16),
            pltpu.VMEM((TABLE, FEAT), F32),
            pltpu.VMEM((NR, 8, 128), I32),
            pltpu.VMEM((NR, 8, 128), I32),
            pltpu.SMEM((NR, 128), I32),
            pltpu.VMEM((CAP, FEAT), F32),
            pltpu.VMEM((NR, CAP, FEAT), BF16),
            pltpu.VMEM((NR, CAP, FEAT), BF16),
            pltpu.VMEM((ROWS, NR * CAP), BF16),
            pltpu.VMEM((NR * CAP, ROWS), BF16),
            pltpu.VMEM((ROWS, CODES), F32),
            pltpu.VMEM((ROWS, CODES), BF16),
            pltpu.VMEM((CODES, ROWS), BF16),
            pltpu.VMEM((8, 128), F32),
            pltpu.VMEM((NC, 8, 128), F32),
            pltpu.VMEM((NZ, ROWS, FEAT), BF16),
            pltpu.VMEM((NZ, ROWS, FEAT), BF16),
            pltpu.VMEM((NZ, ROWS, FEAT), BF16),
            pltpu.VMEM((2, 4, 2, HALF, FEAT), BF16),
            pltpu.VMEM((NR, CODES, FEAT), BF16),
            pltpu.VMEM((2, 5, 2, 128, FEAT), BF16),
            pltpu.VMEM((2, 5, 2, 256, FEAT), BF16),
            pltpu.VMEM((NR, CAP, FEAT), BF16),
            pltpu.SemaphoreType.DMA((4,)),
            pltpu.SemaphoreType.DMA((N_IDS,)),
            pltpu.SemaphoreType.DMA((N_IDS,)),
        ],
        compiler_params=pltpu.CompilerParams(
            collective_id=0, has_side_effects=True, vmem_limit_bytes=60 * 1024 * 1024
        ),
        name="exchange_and_gradients",
    )(hidden_rows, code_table, labels.reshape(4, 128), targets.reshape(4, 128), sub_codebook)
    grad_codes = pl.pallas_call(
        scatter_kernel,
        grid=(TABLE // 256,),
        in_specs=[
            pl.BlockSpec((NR * CAP, FEAT), lambda i: (0, 0)),
            pl.BlockSpec((1, NR * CAP), lambda i: (0, 0)),
        ],
        out_specs=pl.BlockSpec((256, FEAT), lambda i: (i, 0)),
        out_shape=jax.ShapeDtypeStruct((TABLE, FEAT), BF16),
        name="grad_codes",
    )(returned.reshape(NR * CAP, FEAT), asked[:, :CAP].reshape(1, NR * CAP))
    return loss.reshape(ROWS), grad_hidden, grad_codes, grad_sub


def solution(mesh):
    return jax.shard_map(
        per_device,
        mesh=mesh,
        in_specs=(P("row", "col"), P("row", "col"), P("row"), P("row"), P("row", "col")),
        out_specs=(P("row"), P("row", "col"), P("row", "col"), P("row", "col")),
        check_vma=False,
    )
```

```python
import jax
import jax.numpy as jnp
from jax import lax
from jax.experimental import pallas as pl
from jax.experimental.pallas import tpu as pltpu
from jax.sharding import PartitionSpec as P

MESH = pl.DeviceIdType.MESH
F32, BF16, I32 = jnp.float32, jnp.bfloat16, jnp.int32

NX, NY, NZ = 4, 4, 8
NR, NC = NX * NY, 2 * NZ
ROWS, FEAT, CODES = 512, 256, 512
HALF = 256
TABLE = 8192
CAP = 64
CHUNK = 1024
TILE = 2048
NT = (((1,), (1,)), ((), ()))


class Ids:
    def __init__(self):
        self.at = {}
        for name in ("want", "serve0", "serve1", "stat", "ret0", "ret1"):
            for rel in range(16):
                self((name, rel))
        for half in range(2):
            for j in range(5):
                for part in range(4):
                    self(("w", half, j, part))
                    self(("x", half, j, part))
        for way in (1, -1):
            for s in range(4):
                for h in range(2):
                    self(("q", way, s + 1, h))
                    self(("z", way, s, h))
        for dz in range(NZ):
            self(("gs", dz))
            for h in range(2):
                self(("qs", dz, h))

    def __call__(self, name):
        return self.at.setdefault(name, len(self.at))


IDS = Ids()
N_IDS = len(IDS.at)


def dot(a, b, dims=(((1,), (0,)), ((), ()))):
    return lax.dot_general(a, b, dims, preferred_element_type=F32)


def main_kernel(
    hid, table, lab, tgt, wsub,
    loss_o, gh_o, gs_o, ret_o, ask_o,
    wf, qf, tb, tf, wbuf, askv, askr, asks, srv32, srv, fet, pm, mm, tw, lg, dl, dlt,
    stat_s, stat_r, gqo, gqs, sibr, zr, gt, xq, xl, ghb, outb,
    lsem, tsem, ssem, rsem,
):
    row = lax.axis_index("row")
    col = lax.axis_index("col")
    x, y = row // NY, row % NY
    z, k = col // 2, col % 2

    def rdev(r):
        return (r, col)

    def cdev(c):
        return (row, c)

    def xn(d):
        return rdev(((x + d + NX) % NX) * NY + y)

    def yn(d):
        return rdev(x * NY + (y + d + NY) % NY)

    def zn(d):
        return cdev(((z + d + NZ) % NZ) * 2 + k)

    sib = cdev(z * 2 + 1 - k)

    def slot(dx, dy):
        return ((x + dx) % NX) * NY + (y + dy) % NY

    def cp(i, src, dst, dev):
        return pltpu.make_async_remote_copy(
            src_ref=src, dst_ref=dst, send_sem=ssem.at[i], recv_sem=rsem.at[i],
            device_id=dev, device_id_type=MESH,
        )

    sent = []

    def send(name, src, dst, dev):
        c = cp(IDS(name), src, dst, dev)
        c.start()
        sent.append(c)

    def recv(name, dst):
        cp(IDS(name), dst, dst, sib).wait_recv()

    own_w = pltpu.make_async_copy(wsub, wf.at[row], lsem.at[0])
    own_w.start()

    def table_copy(i):
        return pltpu.make_async_copy(
            table.at[pl.ds(i * CHUNK, CHUNK), :], tb.at[i], tsem.at[i]
        )

    for i in range(TABLE // CHUNK):
        table_copy(i).start()

    barrier = pltpu.get_barrier_semaphore()
    for rel in range(1, 16):
        pl.semaphore_signal(barrier, inc=1, device_id=rdev((row + rel) % NR), device_id_type=MESH)
        pl.semaphore_signal(barrier, inc=1, device_id=cdev((col + rel) % NC), device_id_type=MESH)

    lab_row = jnp.concatenate([lab[i:i + 1, :] for i in range(4)], axis=1)
    owner = lax.shift_right_logical(lab_row, 13)
    off = lab_row & (TABLE - 1)
    member = (owner == lax.broadcasted_iota(I32, (NR, ROWS), 0)).astype(F32)
    before = (
        lax.broadcasted_iota(I32, (ROWS, ROWS), 0) < lax.broadcasted_iota(I32, (ROWS, ROWS), 1)
    ).astype(F32).astype(BF16)
    rank = jnp.sum(member * dot(member.astype(BF16), before), axis=0, keepdims=True)
    rank = rank.astype(I32)
    at_rank = (rank == lax.broadcasted_iota(I32, (128, ROWS), 0)).astype(F32).astype(BF16)
    hi = lax.shift_right_logical(off, 7).astype(F32)
    lo = (off & 127).astype(F32)
    both = jnp.concatenate([member * hi, member * lo], axis=0).astype(BF16)
    spread = dot(both, at_rank, NT)
    wanted = (spread[:NR] * 128.0 + spread[NR:]).astype(I32)
    for g in range(NR):
        wbuf[g] = jnp.broadcast_to(wanted[g:g + 1, :], (8, 128))
    place = owner * CAP + rank

    pl.semaphore_wait(barrier, 30)
    for rel in range(1, NR):
        to = (row + rel) % NR
        send(("want", rel), wbuf.at[to], askv.at[row], rdev(to))
    own_w.wait()

    def whalf(s, half, a=0, n=128):
        return wf.at[s, pl.ds(half * 128 + a, n), :]

    def wring(half, j):
        if j == 4:
            return (xn, lambda d: slot(d, 0)) if half == 0 else (yn, lambda d: slot(0, d))
        if half == 0:
            return yn, lambda d: slot(j, d)
        return xn, lambda d: slot(d, j)

    def w_own(half, j):
        nb, at = wring(half, j)
        send(("w", half, j, 0), whalf(at(0), half), whalf(at(0), half), nb(1))
        send(("w", half, j, 1), whalf(at(0), half), whalf(at(0), half), nb(-1))

    def w_mid(half, j, side):
        nb, at = wring(half, j)
        s = at(3) if side == 0 else at(1)
        recv(("w", half, j, side), whalf(s, half))
        part = whalf(s, half, 64 * side, 64)
        send(("w", half, j, 2 + side), part, part, nb(1 - 2 * side))

    def w_last(half, j):
        nb, at = wring(half, j)
        for side in range(2):
            recv(("w", half, j, 2 + side), whalf(at(2), half, 64 * side, 64))

    for half in range(2):
        w_own(half, 4)
    for half in range(2):
        w_own(half, 0)

    for i in range(TABLE // CHUNK):
        table_copy(i).wait()

        @pl.loop(0, CHUNK // 128)
        def _(t, i=i):
            v = tb[i, pl.ds(t * 128, 128), :].astype(F32)
            for h in range(2):
                tf[h, pl.ds(i * CHUNK + t * 128, 128), :] = v[:, h * 128:(h + 1) * 128]

    place_f = place.astype(F32)
    lane = lax.broadcasted_iota(I32, (128, 128), 1)
    for i in range(4):
        wide = jnp.broadcast_to(place_f[:, i * 128:(i + 1) * 128], (128, 128)).T.astype(I32)
        for t in range(8):
            pm[i * 128:(i + 1) * 128, t * 128:(t + 1) * 128] = (
                wide == lane + t * 128
            ).astype(F32).astype(BF16)

    askv[row] = wbuf[row]
    for rel in range(1, NR):
        recv(("want", rel), askv.at[(row - rel + NR) % NR])
    for r in range(NR):
        askr[r:r + 1, :] = askv[r, 0:1, :]
    to_smem = pltpu.make_async_copy(askr, asks, lsem.at[1])
    to_smem.start()
    to_smem.wait()

    def gather(h, r):
        @pl.loop(0, CAP // 16)
        def _(t):
            for u in range(16):
                i = asks[r, t * 16 + u] & (TABLE - 1)
                srv32[pl.ds(t * 16 + u, 1), :] = tf[h, pl.ds(i, 1), :]

    for h in range(2):
        @pl.loop(1, NR)
        def _(rel, h=h):
            to = (row + rel) % NR
            gather(h, to)
            srv[h, to] = srv32[...].astype(BF16)
            cp(IDS((f"serve{h}", 0)) + rel, srv.at[h, to], fet.at[h, row], rdev(to)).start()

        gather(h, row)
        fet[h, row] = srv32[...].astype(BF16)

    for half in range(2):
        for side in range(2):
            w_mid(half, 4, side)
            w_own(half, 3 - 2 * side)
    for half in range(2):
        for side in range(2):
            w_mid(half, 0, side)

    def qpart(s, h):
        return qf.at[s, h]

    for h in range(2):
        for rel in range(1, NR):
            recv((f"serve{h}", rel), fet.at[h, (row - rel + NR) % NR])
        code = dot(pm[...], fet[h].reshape(NR * CAP, 128))
        qf[col, h] = (hid[:, h * 128:(h + 1) * 128].astype(F32) + code).astype(BF16)
        for way in (1, -1):
            send(("q", way, 1, h), qpart(col, h), qpart(col, h), zn(way))
        send(("qs", 0, h), qpart(col, h), qpart(col, h), sib)

    def q_step(s):
        for h in range(2):
            for way in (1, -1):
                if s == 4 and (way == 1) != (h == 0):
                    continue
                at = ((z - way * s + NZ) % NZ) * 2 + k
                piece = qpart(at, h)
                recv(("q", way, s, h), piece)
                if s < 3 or (s == 3 and (way == 1) == (h == 0)):
                    send(("q", way, s + 1, h), piece, piece, zn(way))
                send(("qs", (-way * s) % NZ, h), piece, piece, sib)

    def logits_of(n_ways, s):
        for dz in ([s, NZ - s] if 0 < s < 4 else [s]):
            for h in range(2):
                recv(("qs", dz, h), qpart(((z + dz) % NZ) * 2 + 1 - k, h))

        @pl.loop(0, 2 * n_ways)
        def _(t):
            dz = jnp.where(t % n_ways == 0, s, NZ - s)
            core = t // n_ways
            at = ((z + dz) % NZ) * 2 + core
            for h in range(2):
                rows = pl.ds(h * HALF, HALF)
                q = jnp.concatenate([qf[at, 0, rows, :], qf[at, 1, rows, :]], axis=1)
                lg[rows, :] += dot(q, wf[at])

    for half in range(2):
        w_last(half, 4)
        w_own(half, 2)
    for i in range(4):
        tw[i * 128:(i + 1) * 128, :] = (
            jnp.broadcast_to(tgt[i:i + 1, :].astype(F32), (128, 128)).T.astype(I32) - col * CODES
        )
    for t in range(8):
        mm[t * 128:(t + 1) * 128, :] = (
            place == lax.broadcasted_iota(I32, (128, ROWS), 0) + t * 128
        ).astype(F32).astype(BF16)
    q_step(1)
    for j in (3, 1):
        for half in range(2):
            for side in range(2):
                w_mid(half, j, side)
    q_step(2)
    for half in range(2):
        for side in range(2):
            w_mid(half, 2, side)
    for j in (0, 3, 1, 2):
        for half in range(2):
            w_last(half, j)
    lg[...] = jnp.zeros((ROWS, CODES), F32)
    logits_of(1, 0)
    q_step(3)
    logits_of(2, 1)
    logits_of(2, 2)
    q_step(4)
    logits_of(2, 3)
    logits_of(1, 4)

    def hit_of(i, j):
        return tw[i * 128:(i + 1) * 128, :] == lane + j * 128

    for i in range(4):
        rows = slice(i * 128, (i + 1) * 128)
        v = lg[rows, :]
        peak = jnp.max(v, axis=1, keepdims=True)
        log_sum = peak + jnp.log(jnp.sum(jnp.exp(v - peak), axis=1, keepdims=True))
        hits = jnp.concatenate([hit_of(i, j) for j in range(4)], axis=1)
        target = jnp.sum(jnp.where(hits, v, 0.0), axis=1, keepdims=True)
        pair = jnp.where(lane == 0, log_sum, jnp.where(lane == 1, target, 0.0)).T
        stat_s[i:i + 1, :] = pair[0:1, :]
        stat_s[4 + i:5 + i, :] = pair[1:2, :]
    stat_r[col] = stat_s[...]
    for rel in range(1, NC):
        send(("stat", rel), stat_s, stat_r.at[col], cdev((col + rel) % NC))
    for rel in range(1, NC):
        recv(("stat", rel), stat_r.at[(col - rel + NC) % NC])
    logs = stat_r[:, 0:4, :]
    top = jnp.max(logs, axis=0)
    log_total = top + jnp.log(jnp.sum(jnp.exp(logs - top[None]), axis=0))
    loss_o[...] = log_total - jnp.sum(stat_r[:, 4:8, :], axis=0)
    for i in range(4):
        wide = jnp.broadcast_to(log_total[i:i + 1, :], (128, 128)).T
        for j in range(4):
            v = lg[i * 128:(i + 1) * 128, j * 128:(j + 1) * 128]
            d = jnp.exp(v - wide) - hit_of(i, j).astype(F32)
            dl[i * 128:(i + 1) * 128, j * 128:(j + 1) * 128] = d.astype(BF16)
            dlt[j * 128:(j + 1) * 128, i * 128:(i + 1) * 128] = d.T.astype(BF16)

    def sib_block(dz):
        v = dot(dl[...], wf[((z + dz) % NZ) * 2 + 1 - k], NT).astype(BF16)
        for h in range(2):
            gqs[dz, h] = v[:, h * 128:(h + 1) * 128]
        send(("gs", dz), gqs.at[dz], sibr.at[dz], sib)

    def own_block(dz):
        v = dot(dl[...], wf[((z + dz) % NZ) * 2 + k], NT).astype(BF16)
        for h in range(2):
            gqo[dz, h] = v[:, h * 128:(h + 1) * 128]

    def grad_block(dz):
        sib_block(dz)
        own_block(dz)

    def pair_up(dz):
        recv(("gs", dz), sibr.at[dz])
        gqo[dz] = (gqo[dz].astype(F32) + sibr[dz].astype(F32)).astype(BF16)

    def sub_block(dx, dy):
        s = slot(dx, dy)
        gt[s] = dot(dlt[...], jnp.concatenate([qf[s, 0], qf[s, 1]], axis=1)).astype(BF16)

    def zpart(dz, h):
        return gqo.at[dz % NZ, h]

    def zsend(way, d, h):
        send(("z", way, d, h), zpart(way * (d + 1), h), zr.at[(1 - way) // 2, d, h], zn(way))

    def zadd(way, d, h):
        got = zr.at[(1 - way) // 2, d, h]
        recv(("z", way, d, h), got)
        part = zpart(way * d, h)
        part[...] = (part[...].astype(F32) + got[...].astype(F32)).astype(BF16)

    def xring(half, j):
        if j == 4:
            return (xn, lambda d: slot(d, 0)) if half == 0 else (yn, lambda d: slot(0, d))
        if half == 0:
            return yn, lambda d: slot(j, d)
        return xn, lambda d: slot(d, j)

    def xpart(s, half, a=0, n=256):
        return gt.at[s, pl.ds(half * 256 + a, n), :]

    def x_start(half, j):
        nb, at = xring(half, j)
        for side in range(2):
            send(("x", half, j, side), xpart(at(2), half, 128 * side, 128), xq.at[half, j, side], nb(1 - 2 * side))

    def x_mid(half, j):
        nb, at = xring(half, j)
        for side in range(2):
            got = xq.at[half, j, side]
            recv(("x", half, j, side), got)
            s = at(1) if side == 0 else at(3)
            part = xpart(s, half, 128 * side, 128)
            part[...] = (part[...].astype(F32) + got[...].astype(F32)).astype(BF16)
            send(("x", half, j, 2 + side), xpart(s, half), xl.at[half, j, side], nb(1 - 2 * side))

    def x_end(half, j):
        nb, at = xring(half, j)
        for side in range(2):
            recv(("x", half, j, 2 + side), xl.at[half, j, side])
        part = xpart(at(0), half)
        part[...] = (
            part[...].astype(F32) + xl[half, j, 0].astype(F32) + xl[half, j, 1].astype(F32)
        ).astype(BF16)

    sib_block(4)
    sub_block(2, 2)
    for half in range(2):
        x_start(half, 2)
    own_block(4)
    sib_block(3)
    sib_block(5)
    pair_up(4)
    zsend(1, 3, 0)
    zsend(-1, 3, 1)
    own_block(3)
    own_block(5)
    pair_up(3)
    pair_up(5)
    zsend(1, 2, 1)
    zsend(-1, 2, 0)
    for d in (1, 3, 0):
        sub_block(2, d)
        sub_block(d, 2)
        for half in range(2):
            x_start(half, d)
    grad_block(2)
    grad_block(6)
    for half in range(2):
        x_mid(half, 2)
    pair_up(2)
    pair_up(6)
    for way, h in ((1, 0), (-1, 1)):
        zadd(way, 3, h)
        zsend(way, 2, h)
    sub_block(1, 1)
    sub_block(3, 1)
    sub_block(1, 3)
    sub_block(3, 3)
    sub_block(1, 0)
    sub_block(0, 1)
    sub_block(3, 0)
    sub_block(0, 3)
    sub_block(0, 0)
    for j in (1, 3):
        for half in range(2):
            x_mid(half, j)
    for way, h in ((1, 1), (-1, 0)):
        zadd(way, 2, h)
        zsend(way, 1, h)
    grad_block(1)
    grad_block(7)
    grad_block(0)
    for half in range(2):
        x_end(half, 2)
        x_start(half, 4)
    for half in range(2):
        x_mid(half, 0)
    pair_up(1)
    pair_up(7)
    for way, h in ((1, 0), (-1, 1)):
        zadd(way, 2, h)
        zsend(way, 1, h)
    for way, h in ((1, 1), (-1, 0)):
        zadd(way, 1, h)
        zsend(way, 0, h)
    for half in range(2):
        x_end(half, 1)
        x_end(half, 3)
    for half in range(2):
        x_mid(half, 4)
    for way, h in ((1, 0), (-1, 1)):
        zadd(way, 1, h)
        zsend(way, 0, h)
    pair_up(0)
    for half in range(2):
        x_end(half, 0)

    for h in range(2):
        for way in (1, -1):
            recv(("z", way, 0, h), zr.at[(1 - way) // 2, 0, h])
        total = gqo[0, h].astype(F32) + zr[0, 0, h].astype(F32) + zr[1, 0, h].astype(F32)
        ghb[h] = total.astype(BF16)
        gh_o[:, h * 128:(h + 1) * 128] = ghb[h]
        for t in range(4):
            moved = dot(mm[t * 256:(t + 1) * 256, :], ghb[h]).astype(BF16)
            for u in range(4):
                outb[h, 4 * t + u] = moved[u * CAP:(u + 1) * CAP]
        for rel in range(1, NR):
            to = (row + rel) % NR
            send((f"ret{h}", rel), outb.at[h, to], ret_o.at[h, row], rdev(to))
        ret_o[h, row] = outb[h, row]
    for t in range(NR // 2):
        ask_o[t:t + 1, :] = jnp.concatenate(
            [askv[2 * t, 0:1, :CAP], askv[2 * t + 1, 0:1, :CAP]], axis=1
        )
    for half in range(2):
        x_end(half, 4)
    gs_o[...] = gt[row].astype(F32).T.astype(BF16)
    for h in range(2):
        for rel in range(1, NR):
            recv((f"ret{h}", rel), ret_o.at[h, (row - rel + NR) % NR])

    for c in sent:
        c.wait_send()

    for h in range(2):
        @pl.loop(1, NR)
        def _(rel, h=h):
            cp(IDS((f"serve{h}", 0)) + rel, srv.at[h, 0], fet.at[h, 0], sib).wait_send()


def scatter_kernel(ret, ask, gh, gs, loss, codes_o, gh_o, gs_o, loss_o):
    base = pl.program_id(0) * TILE
    rows = jnp.concatenate([ret[h].reshape(NR * CAP, 128) for h in range(2)], axis=1)
    slots = lax.broadcasted_iota(I32, (TILE, 128), 0)
    hits = jnp.concatenate(
        [(ask[t:t + 1, :] - base == slots).astype(F32).astype(BF16) for t in range(8)], axis=1
    )
    codes_o[...] = dot(hits, rows).astype(BF16)
    gh_o[...] = gh[...]
    gs_o[...] = gs[...]
    loss_o[...] = loss[...]


def per_device(hidden_rows, code_table, labels, targets, sub_codebook):
    vmem = pl.BlockSpec(memory_space=pltpu.VMEM)
    loss, grad_hidden, grad_sub, returned, asked = pl.pallas_call(
        main_kernel,
        out_shape=(
            jax.ShapeDtypeStruct((4, 128), F32),
            jax.ShapeDtypeStruct((ROWS, FEAT), BF16),
            jax.ShapeDtypeStruct((FEAT, CODES), BF16),
            jax.ShapeDtypeStruct((2, NR, CAP, 128), BF16),
            jax.ShapeDtypeStruct((8, 128), I32),
        ),
        in_specs=[vmem, pl.BlockSpec(memory_space=pl.ANY), vmem, vmem, vmem],
        out_specs=[vmem] * 5,
        scratch_shapes=[
            pltpu.VMEM((NR, FEAT, CODES), BF16),
            pltpu.VMEM((NC, 2, ROWS, 128), BF16),
            pltpu.VMEM((TABLE // CHUNK, CHUNK, FEAT), BF16),
            pltpu.VMEM((2, TABLE, 128), F32),
            pltpu.VMEM((NR, 8, 128), I32),
            pltpu.VMEM((NR, 8, 128), I32),
            pltpu.VMEM((NR, 128), I32),
            pltpu.SMEM((NR, 128), I32),
            pltpu.VMEM((CAP, 128), F32),
            pltpu.VMEM((2, NR, CAP, 128), BF16),
            pltpu.VMEM((2, NR, CAP, 128), BF16),
            pltpu.VMEM((ROWS, NR * CAP), BF16),
            pltpu.VMEM((NR * CAP, ROWS), BF16),
            pltpu.VMEM((ROWS, 128), I32),
            pltpu.VMEM((ROWS, CODES), F32),
            pltpu.VMEM((ROWS, CODES), BF16),
            pltpu.VMEM((CODES, ROWS), BF16),
            pltpu.VMEM((8, 128), F32),
            pltpu.VMEM((NC, 8, 128), F32),
            pltpu.VMEM((NZ, 2, ROWS, 128), BF16),
            pltpu.VMEM((NZ, 2, ROWS, 128), BF16),
            pltpu.VMEM((NZ, 2, ROWS, 128), BF16),
            pltpu.VMEM((2, 4, 2, ROWS, 128), BF16),
            pltpu.VMEM((NR, CODES, FEAT), BF16),
            pltpu.VMEM((2, 5, 2, 128, FEAT), BF16),
            pltpu.VMEM((2, 5, 2, 256, FEAT), BF16),
            pltpu.VMEM((2, ROWS, 128), BF16),
            pltpu.VMEM((2, NR, CAP, 128), BF16),
            pltpu.SemaphoreType.DMA((2,)),
            pltpu.SemaphoreType.DMA((TABLE // CHUNK,)),
            pltpu.SemaphoreType.DMA((N_IDS,)),
            pltpu.SemaphoreType.DMA((N_IDS,)),
        ],
        compiler_params=pltpu.CompilerParams(
            collective_id=0, has_side_effects=True, vmem_limit_bytes=60 * 1024 * 1024
        ),
        name="exchange_and_gradients",
    )(hidden_rows, code_table, labels.reshape(4, 128), targets.reshape(4, 128), sub_codebook)
    steps = TABLE // TILE
    grad_codes, grad_hidden, grad_sub, loss = pl.pallas_call(
        scatter_kernel,
        grid=(steps,),
        in_specs=[
            pl.BlockSpec((2, NR, CAP, 128), lambda i: (0, 0, 0, 0)),
            pl.BlockSpec((8, 128), lambda i: (0, 0)),
            pl.BlockSpec((ROWS // steps, FEAT), lambda i: (i, 0)),
            pl.BlockSpec((FEAT // steps, CODES), lambda i: (i, 0)),
            pl.BlockSpec((4, 128), lambda i: (0, 0)),
        ],
        out_specs=[
            pl.BlockSpec((TILE, FEAT), lambda i: (i, 0)),
            pl.BlockSpec((ROWS // steps, FEAT), lambda i: (i, 0)),
            pl.BlockSpec((FEAT // steps, CODES), lambda i: (i, 0)),
            pl.BlockSpec((4, 128), lambda i: (0, 0)),
        ],
        out_shape=[
            jax.ShapeDtypeStruct((TABLE, FEAT), BF16),
            jax.ShapeDtypeStruct((ROWS, FEAT), BF16),
            jax.ShapeDtypeStruct((FEAT, CODES), BF16),
            jax.ShapeDtypeStruct((4, 128), F32),
        ],
        compiler_params=pltpu.CompilerParams(vmem_limit_bytes=50 * 1024 * 1024),
        name="grad_codes",
    )(returned, asked, grad_hidden, grad_sub, loss)
    return loss.reshape(ROWS), grad_hidden, grad_codes, grad_sub


def solution(mesh):
    return jax.shard_map(
        per_device,
        mesh=mesh,
        in_specs=(P("row", "col"), P("row", "col"), P("row"), P("row"), P("row", "col")),
        out_specs=(P("row"), P("row", "col"), P("row", "col"), P("row", "col")),
        check_vma=False,
    )
```

```python
import jax
import jax.numpy as jnp
from jax import lax
from jax.experimental import pallas as pl
from jax.experimental.pallas import tpu as pltpu
from jax.sharding import PartitionSpec as P

MESH = pl.DeviceIdType.MESH
F32, BF16, I32 = jnp.float32, jnp.bfloat16, jnp.int32

NX, NY, NZ = 4, 4, 8
NR, NC = NX * NY, 2 * NZ
ROWS, FEAT, CODES = 512, 256, 512
HALF = 256
TABLE = 8192
CAP = 64
CHUNK = 1024
TILE = 2048
NT = (((1,), (1,)), ((), ()))


class Ids:
    def __init__(self):
        self.at = {}
        for name in ("want", "serve0", "serve1", "stat", "ret0", "ret1"):
            for rel in range(16):
                self((name, rel))
        for half in range(2):
            for j in range(5):
                for part in range(4):
                    self(("w", half, j, part))
                    self(("x", half, j, part))
        for way in (1, -1):
            for s in range(4):
                for h in range(2):
                    self(("q", way, s + 1, h))
                    self(("z", way, s, h))
        for dz in range(NZ):
            self(("gs", dz))
            for h in range(2):
                self(("qs", dz, h))

    def __call__(self, name):
        return self.at.setdefault(name, len(self.at))


IDS = Ids()
N_IDS = len(IDS.at)


def dot(a, b, dims=(((1,), (0,)), ((), ()))):
    return lax.dot_general(a, b, dims, preferred_element_type=F32)


def main_kernel(
    hid, table, lab, tgt, wsub,
    loss_o, gh_o, gs_o, ret_o, ask_o,
    wf, qf, tb, tf, wbuf, askv, askr, asks, srv32, srv, fet, pm, mm, tw, lg, dl, dlt,
    stat_s, stat_r, gqo, gqs, sibr, zr, gt, xq, xl, ghb, outb,
    lsem, tsem, ssem, rsem,
):
    row = lax.axis_index("row")
    col = lax.axis_index("col")
    x, y = row // NY, row % NY
    z, k = col // 2, col % 2

    def rdev(r):
        return (r, col)

    def cdev(c):
        return (row, c)

    def xn(d):
        return rdev(((x + d + NX) % NX) * NY + y)

    def yn(d):
        return rdev(x * NY + (y + d + NY) % NY)

    def zn(d):
        return cdev(((z + d + NZ) % NZ) * 2 + k)

    sib = cdev(z * 2 + 1 - k)

    def slot(dx, dy):
        return ((x + dx) % NX) * NY + (y + dy) % NY

    def cp(i, src, dst, dev):
        return pltpu.make_async_remote_copy(
            src_ref=src, dst_ref=dst, send_sem=ssem.at[i], recv_sem=rsem.at[i],
            device_id=dev, device_id_type=MESH,
        )

    sent = []

    def send(name, src, dst, dev):
        c = cp(IDS(name), src, dst, dev)
        c.start()
        sent.append(c)

    def recv(name, dst):
        cp(IDS(name), dst, dst, sib).wait_recv()

    own_w = pltpu.make_async_copy(wsub, wf.at[row], lsem.at[0])
    own_w.start()

    def table_copy(i):
        return pltpu.make_async_copy(
            table.at[pl.ds(i * CHUNK, CHUNK), :], tb.at[i], tsem.at[i]
        )

    for i in range(TABLE // CHUNK):
        table_copy(i).start()

    barrier = pltpu.get_barrier_semaphore()
    for rel in range(1, 16):
        pl.semaphore_signal(barrier, inc=1, device_id=rdev((row + rel) % NR), device_id_type=MESH)
        pl.semaphore_signal(barrier, inc=1, device_id=cdev((col + rel) % NC), device_id_type=MESH)

    lab_row = jnp.concatenate([lab[i:i + 1, :] for i in range(4)], axis=1)
    owner = lax.shift_right_logical(lab_row, 13)
    off = lab_row & (TABLE - 1)
    member = (owner == lax.broadcasted_iota(I32, (NR, ROWS), 0)).astype(F32)
    before = (
        lax.broadcasted_iota(I32, (ROWS, ROWS), 0) < lax.broadcasted_iota(I32, (ROWS, ROWS), 1)
    ).astype(F32).astype(BF16)
    rank = jnp.sum(member * dot(member.astype(BF16), before), axis=0, keepdims=True)
    rank = rank.astype(I32)
    at_rank = (rank == lax.broadcasted_iota(I32, (128, ROWS), 0)).astype(F32).astype(BF16)
    hi = lax.shift_right_logical(off, 7).astype(F32)
    lo = (off & 127).astype(F32)
    both = jnp.concatenate([member * hi, member * lo], axis=0).astype(BF16)
    spread = dot(both, at_rank, NT)
    wanted = (spread[:NR] * 128.0 + spread[NR:]).astype(I32)
    for g in range(NR):
        wbuf[g] = jnp.broadcast_to(wanted[g:g + 1, :], (8, 128))
    place = owner * CAP + rank

    pl.semaphore_wait(barrier, 30)
    for rel in range(1, NR):
        to = (row + rel) % NR
        send(("want", rel), wbuf.at[to], askv.at[row], rdev(to))
    own_w.wait()

    def whalf(s, half, a=0, n=128):
        return wf.at[s, pl.ds(half * 128 + a, n), :]

    def wring(half, j):
        if j == 4:
            return (xn, lambda d: slot(d, 0)) if half == 0 else (yn, lambda d: slot(0, d))
        if half == 0:
            return yn, lambda d: slot(j, d)
        return xn, lambda d: slot(d, j)

    def w_own(half, j):
        nb, at = wring(half, j)
        send(("w", half, j, 0), whalf(at(0), half), whalf(at(0), half), nb(1))
        send(("w", half, j, 1), whalf(at(0), half), whalf(at(0), half), nb(-1))

    def w_mid(half, j, side):
        nb, at = wring(half, j)
        s = at(3) if side == 0 else at(1)
        recv(("w", half, j, side), whalf(s, half))
        part = whalf(s, half, 64 * side, 64)
        send(("w", half, j, 2 + side), part, part, nb(1 - 2 * side))

    def w_last(half, j):
        nb, at = wring(half, j)
        for side in range(2):
            recv(("w", half, j, 2 + side), whalf(at(2), half, 64 * side, 64))

    for half in range(2):
        w_own(half, 4)
    for half in range(2):
        w_own(half, 0)

    for i in range(TABLE // CHUNK):
        table_copy(i).wait()

        @pl.loop(0, CHUNK // 128)
        def _(t, i=i):
            v = tb[i, pl.ds(t * 128, 128), :].astype(F32)
            for h in range(2):
                tf[h, pl.ds(i * CHUNK + t * 128, 128), :] = v[:, h * 128:(h + 1) * 128]

    place_f = place.astype(F32)
    lane = lax.broadcasted_iota(I32, (128, 128), 1)
    for i in range(4):
        wide = jnp.broadcast_to(place_f[:, i * 128:(i + 1) * 128], (128, 128)).T.astype(I32)
        for t in range(8):
            pm[i * 128:(i + 1) * 128, t * 128:(t + 1) * 128] = (
                wide == lane + t * 128
            ).astype(F32).astype(BF16)

    askv[row] = wbuf[row]
    for rel in range(1, NR):
        recv(("want", rel), askv.at[(row - rel + NR) % NR])
    for r in range(NR):
        askr[r:r + 1, :] = askv[r, 0:1, :]
    to_smem = pltpu.make_async_copy(askr, asks, lsem.at[1])
    to_smem.start()
    to_smem.wait()

    def gather(r):
        @pl.loop(0, CAP // 16)
        def _(t):
            picks = [asks[r, t * 16 + u] & (TABLE - 1) for u in range(16)]
            rows = [(tf[0, pl.ds(i, 1), :], tf[1, pl.ds(i, 1), :]) for i in picks]
            for u in range(16):
                for h in range(2):
                    srv32[h, pl.ds(t * 16 + u, 1), :] = rows[u][h]

    def serve(h, rel):
        to = (row + rel) % NR
        cp(IDS((f"serve{h}", 0)) + rel, srv.at[h, to], fet.at[h, row], rdev(to)).start()

    @pl.loop(1, NR)
    def _(rel):
        to = (row + rel) % NR
        gather(to)
        for h in range(2):
            srv[h, to] = srv32[h].astype(BF16)
        serve(0, rel)

    @pl.loop(1, NR)
    def _(rel):
        serve(1, rel)

    gather(row)
    for h in range(2):
        fet[h, row] = srv32[h].astype(BF16)

    for half in range(2):
        for side in range(2):
            w_mid(half, 4, side)
            w_own(half, 3 - 2 * side)
    for half in range(2):
        for side in range(2):
            w_mid(half, 0, side)

    def qpart(s, h):
        return qf.at[s, h]

    for h in range(2):
        for rel in range(1, NR):
            recv((f"serve{h}", rel), fet.at[h, (row - rel + NR) % NR])
        code = dot(pm[...], fet[h].reshape(NR * CAP, 128))
        qf[col, h] = (hid[:, h * 128:(h + 1) * 128].astype(F32) + code).astype(BF16)
        send(("qs", 0, h), qpart(col, h), qpart(col, h), sib)
        for way in (1, -1):
            send(("q", way, 1, h), qpart(col, h), qpart(col, h), zn(way))

    def q_step(s, h):
        for way in (1, -1):
            if s == 4 and (way == 1) != (h == 0):
                continue
            at = ((z - way * s + NZ) % NZ) * 2 + k
            piece = qpart(at, h)
            recv(("q", way, s, h), piece)
            send(("qs", (-way * s) % NZ, h), piece, piece, sib)
            if s < 3 or (s == 3 and (way == 1) == (h == 0)):
                send(("q", way, s + 1, h), piece, piece, zn(way))

    def logits_of(n_ways, s):
        for dz in ([s, NZ - s] if 0 < s < 4 else [s]):
            for h in range(2):
                recv(("qs", dz, h), qpart(((z + dz) % NZ) * 2 + 1 - k, h))

        @pl.loop(0, 2 * n_ways)
        def _(t):
            dz = jnp.where(t % n_ways == 0, s, NZ - s)
            core = t // n_ways
            at = ((z + dz) % NZ) * 2 + core
            for h in range(2):
                rows = pl.ds(h * HALF, HALF)
                q = jnp.concatenate([qf[at, 0, rows, :], qf[at, 1, rows, :]], axis=1)
                lg[rows, :] += dot(q, wf[at])

    for half in range(2):
        w_last(half, 4)
        w_own(half, 2)
    for j in (3, 1):
        for half in range(2):
            for side in range(2):
                w_mid(half, j, side)
    for i in range(4):
        tw[i * 128:(i + 1) * 128, :] = (
            jnp.broadcast_to(tgt[i:i + 1, :].astype(F32), (128, 128)).T.astype(I32) - col * CODES
        )
    for t in range(8):
        mm[t * 128:(t + 1) * 128, :] = (
            place == lax.broadcasted_iota(I32, (128, ROWS), 0) + t * 128
        ).astype(F32).astype(BF16)
    lg[...] = jnp.zeros((ROWS, CODES), F32)
    for h in range(2):
        q_step(1, h)
    for half in range(2):
        for side in range(2):
            w_mid(half, 2, side)
    for h in range(2):
        q_step(2, h)
    for j in (0, 3, 1, 2):
        for half in range(2):
            w_last(half, j)
    logits_of(1, 0)
    q_step(3, 0)
    logits_of(2, 1)
    q_step(3, 1)
    logits_of(2, 2)
    for h in range(2):
        q_step(4, h)
    logits_of(2, 3)
    logits_of(1, 4)

    def hit_of(i, j):
        return tw[i * 128:(i + 1) * 128, :] == lane + j * 128

    for i in range(4):
        rows = slice(i * 128, (i + 1) * 128)
        v = lg[rows, :]
        peak = jnp.max(v, axis=1, keepdims=True)
        log_sum = peak + jnp.log(jnp.sum(jnp.exp(v - peak), axis=1, keepdims=True))
        hits = jnp.concatenate([hit_of(i, j) for j in range(4)], axis=1)
        target = jnp.sum(jnp.where(hits, v, 0.0), axis=1, keepdims=True)
        pair = jnp.where(lane == 0, log_sum, jnp.where(lane == 1, target, 0.0)).T
        stat_s[i:i + 1, :] = pair[0:1, :]
        stat_s[4 + i:5 + i, :] = pair[1:2, :]
    stat_r[col] = stat_s[...]
    for rel in range(1, NC):
        send(("stat", rel), stat_s, stat_r.at[col], cdev((col + rel) % NC))
    for rel in range(1, NC):
        recv(("stat", rel), stat_r.at[(col - rel + NC) % NC])
    logs = stat_r[:, 0:4, :]
    top = jnp.max(logs, axis=0)
    log_total = top + jnp.log(jnp.sum(jnp.exp(logs - top[None]), axis=0))
    loss_o[...] = log_total - jnp.sum(stat_r[:, 4:8, :], axis=0)
    for i in range(4):
        wide = jnp.broadcast_to(log_total[i:i + 1, :], (128, 128)).T
        for j in range(4):
            v = lg[i * 128:(i + 1) * 128, j * 128:(j + 1) * 128]
            d = jnp.exp(v - wide) - hit_of(i, j).astype(F32)
            dl[i * 128:(i + 1) * 128, j * 128:(j + 1) * 128] = d.astype(BF16)
            dlt[j * 128:(j + 1) * 128, i * 128:(i + 1) * 128] = d.T.astype(BF16)

    def sib_block(dz):
        v = dot(dl[...], wf[((z + dz) % NZ) * 2 + 1 - k], NT).astype(BF16)
        for h in range(2):
            gqs[dz, h] = v[:, h * 128:(h + 1) * 128]
        send(("gs", dz), gqs.at[dz], sibr.at[dz], sib)

    def own_block(dz):
        v = dot(dl[...], wf[((z + dz) % NZ) * 2 + k], NT).astype(BF16)
        for h in range(2):
            gqo[dz, h] = v[:, h * 128:(h + 1) * 128]

    def grad_block(dz):
        sib_block(dz)
        own_block(dz)

    def pair_up(dz):
        recv(("gs", dz), sibr.at[dz])
        gqo[dz] = (gqo[dz].astype(F32) + sibr[dz].astype(F32)).astype(BF16)

    def sub_block(dx, dy):
        s = slot(dx, dy)
        gt[s] = dot(dlt[...], jnp.concatenate([qf[s, 0], qf[s, 1]], axis=1)).astype(BF16)

    def zpart(dz, h):
        return gqo.at[dz % NZ, h]

    def zsend(way, d, h):
        send(("z", way, d, h), zpart(way * (d + 1), h), zr.at[(1 - way) // 2, d, h], zn(way))

    def zadd(way, d, h):
        got = zr.at[(1 - way) // 2, d, h]
        recv(("z", way, d, h), got)
        part = zpart(way * d, h)
        part[...] = (part[...].astype(F32) + got[...].astype(F32)).astype(BF16)

    def xring(half, j):
        if j == 4:
            return (xn, lambda d: slot(d, 0)) if half == 0 else (yn, lambda d: slot(0, d))
        if half == 0:
            return yn, lambda d: slot(j, d)
        return xn, lambda d: slot(d, j)

    def xpart(s, half, a=0, n=256):
        return gt.at[s, pl.ds(half * 256 + a, n), :]

    def x_start(half, j):
        nb, at = xring(half, j)
        for side in range(2):
            send(("x", half, j, side), xpart(at(2), half, 128 * side, 128), xq.at[half, j, side], nb(1 - 2 * side))

    def x_mid(half, j):
        nb, at = xring(half, j)
        for side in range(2):
            got = xq.at[half, j, side]
            recv(("x", half, j, side), got)
            s = at(1) if side == 0 else at(3)
            part = xpart(s, half, 128 * side, 128)
            part[...] = (part[...].astype(F32) + got[...].astype(F32)).astype(BF16)
            send(("x", half, j, 2 + side), xpart(s, half), xl.at[half, j, side], nb(1 - 2 * side))

    def x_end(half, j):
        nb, at = xring(half, j)
        for side in range(2):
            recv(("x", half, j, 2 + side), xl.at[half, j, side])
        part = xpart(at(0), half)
        part[...] = (
            part[...].astype(F32) + xl[half, j, 0].astype(F32) + xl[half, j, 1].astype(F32)
        ).astype(BF16)

    sib_block(4)
    sub_block(2, 2)
    for half in range(2):
        x_start(half, 2)
    own_block(4)
    sib_block(3)
    sib_block(5)
    pair_up(4)
    zsend(1, 3, 0)
    zsend(-1, 3, 1)
    own_block(3)
    own_block(5)
    pair_up(3)
    pair_up(5)
    zsend(1, 2, 1)
    zsend(-1, 2, 0)
    for d in (1, 3, 0):
        sub_block(2, d)
        sub_block(d, 2)
        for half in range(2):
            x_start(half, d)
    grad_block(2)
    grad_block(6)
    for half in range(2):
        x_mid(half, 2)
    pair_up(2)
    pair_up(6)
    for way, h in ((1, 0), (-1, 1)):
        zadd(way, 3, h)
        zsend(way, 2, h)
    sub_block(1, 1)
    sub_block(3, 1)
    sub_block(1, 3)
    sub_block(3, 3)
    sub_block(1, 0)
    sub_block(0, 1)
    sub_block(3, 0)
    sub_block(0, 3)
    sub_block(0, 0)
    for j in (1, 3):
        for half in range(2):
            x_mid(half, j)
    for way, h in ((1, 1), (-1, 0)):
        zadd(way, 2, h)
        zsend(way, 1, h)
    grad_block(1)
    grad_block(7)
    grad_block(0)
    for half in range(2):
        x_end(half, 2)
        x_start(half, 4)
    for half in range(2):
        x_mid(half, 0)
    pair_up(1)
    pair_up(7)
    for way, h in ((1, 0), (-1, 1)):
        zadd(way, 2, h)
        zsend(way, 1, h)
    for way, h in ((1, 1), (-1, 0)):
        zadd(way, 1, h)
        zsend(way, 0, h)
    for half in range(2):
        x_end(half, 1)
        x_end(half, 3)
    for half in range(2):
        x_mid(half, 4)
    for way, h in ((1, 0), (-1, 1)):
        zadd(way, 1, h)
        zsend(way, 0, h)
    pair_up(0)
    for half in range(2):
        x_end(half, 0)

    for h in range(2):
        for way in (1, -1):
            recv(("z", way, 0, h), zr.at[(1 - way) // 2, 0, h])
        total = gqo[0, h].astype(F32) + zr[0, 0, h].astype(F32) + zr[1, 0, h].astype(F32)
        ghb[h] = total.astype(BF16)
        gh_o[:, h * 128:(h + 1) * 128] = ghb[h]
        for t in range(4):
            moved = dot(mm[t * 256:(t + 1) * 256, :], ghb[h]).astype(BF16)
            for u in range(4):
                outb[h, 4 * t + u] = moved[u * CAP:(u + 1) * CAP]
        for rel in range(1, NR):
            to = (row + rel) % NR
            send((f"ret{h}", rel), outb.at[h, to], ret_o.at[h, row], rdev(to))
        ret_o[h, row] = outb[h, row]
    for t in range(NR // 2):
        ask_o[t:t + 1, :] = jnp.concatenate(
            [askv[2 * t, 0:1, :CAP], askv[2 * t + 1, 0:1, :CAP]], axis=1
        )
    for half in range(2):
        x_end(half, 4)
    gs_o[...] = gt[row].astype(F32).T.astype(BF16)
    for h in range(2):
        for rel in range(1, NR):
            recv((f"ret{h}", rel), ret_o.at[h, (row - rel + NR) % NR])

    for c in sent:
        c.wait_send()

    for h in range(2):
        @pl.loop(1, NR)
        def _(rel, h=h):
            cp(IDS((f"serve{h}", 0)) + rel, srv.at[h, 0], fet.at[h, 0], sib).wait_send()


def scatter_kernel(ret, ask, gh, gs, loss, codes_o, gh_o, gs_o, loss_o):
    base = pl.program_id(0) * TILE
    rows = jnp.concatenate([ret[h].reshape(NR * CAP, 128) for h in range(2)], axis=1)
    slots = lax.broadcasted_iota(I32, (TILE, 128), 0)
    hits = jnp.concatenate(
        [(ask[t:t + 1, :] - base == slots).astype(F32).astype(BF16) for t in range(8)], axis=1
    )
    codes_o[...] = dot(hits, rows).astype(BF16)
    gh_o[...] = gh[...]
    gs_o[...] = gs[...]
    loss_o[...] = loss[...]


def per_device(hidden_rows, code_table, labels, targets, sub_codebook):
    vmem = pl.BlockSpec(memory_space=pltpu.VMEM)
    loss, grad_hidden, grad_sub, returned, asked = pl.pallas_call(
        main_kernel,
        out_shape=(
            jax.ShapeDtypeStruct((4, 128), F32),
            jax.ShapeDtypeStruct((ROWS, FEAT), BF16),
            jax.ShapeDtypeStruct((FEAT, CODES), BF16),
            jax.ShapeDtypeStruct((2, NR, CAP, 128), BF16),
            jax.ShapeDtypeStruct((8, 128), I32),
        ),
        in_specs=[vmem, pl.BlockSpec(memory_space=pl.ANY), vmem, vmem, vmem],
        out_specs=[vmem] * 5,
        scratch_shapes=[
            pltpu.VMEM((NR, FEAT, CODES), BF16),
            pltpu.VMEM((NC, 2, ROWS, 128), BF16),
            pltpu.VMEM((TABLE // CHUNK, CHUNK, FEAT), BF16),
            pltpu.VMEM((2, TABLE, 128), F32),
            pltpu.VMEM((NR, 8, 128), I32),
            pltpu.VMEM((NR, 8, 128), I32),
            pltpu.VMEM((NR, 128), I32),
            pltpu.SMEM((NR, 128), I32),
            pltpu.VMEM((2, CAP, 128), F32),
            pltpu.VMEM((2, NR, CAP, 128), BF16),
            pltpu.VMEM((2, NR, CAP, 128), BF16),
            pltpu.VMEM((ROWS, NR * CAP), BF16),
            pltpu.VMEM((NR * CAP, ROWS), BF16),
            pltpu.VMEM((ROWS, 128), I32),
            pltpu.VMEM((ROWS, CODES), F32),
            pltpu.VMEM((ROWS, CODES), BF16),
            pltpu.VMEM((CODES, ROWS), BF16),
            pltpu.VMEM((8, 128), F32),
            pltpu.VMEM((NC, 8, 128), F32),
            pltpu.VMEM((NZ, 2, ROWS, 128), BF16),
            pltpu.VMEM((NZ, 2, ROWS, 128), BF16),
            pltpu.VMEM((NZ, 2, ROWS, 128), BF16),
            pltpu.VMEM((2, 4, 2, ROWS, 128), BF16),
            pltpu.VMEM((NR, CODES, FEAT), BF16),
            pltpu.VMEM((2, 5, 2, 128, FEAT), BF16),
            pltpu.VMEM((2, 5, 2, 256, FEAT), BF16),
            pltpu.VMEM((2, ROWS, 128), BF16),
            pltpu.VMEM((2, NR, CAP, 128), BF16),
            pltpu.SemaphoreType.DMA((2,)),
            pltpu.SemaphoreType.DMA((TABLE // CHUNK,)),
            pltpu.SemaphoreType.DMA((N_IDS,)),
            pltpu.SemaphoreType.DMA((N_IDS,)),
        ],
        compiler_params=pltpu.CompilerParams(
            collective_id=0, has_side_effects=True, vmem_limit_bytes=60 * 1024 * 1024
        ),
        name="exchange_and_gradients",
    )(hidden_rows, code_table, labels.reshape(4, 128), targets.reshape(4, 128), sub_codebook)
    steps = TABLE // TILE
    grad_codes, grad_hidden, grad_sub, loss = pl.pallas_call(
        scatter_kernel,
        grid=(steps,),
        in_specs=[
            pl.BlockSpec((2, NR, CAP, 128), lambda i: (0, 0, 0, 0)),
            pl.BlockSpec((8, 128), lambda i: (0, 0)),
            pl.BlockSpec((ROWS // steps, FEAT), lambda i: (i, 0)),
            pl.BlockSpec((FEAT // steps, CODES), lambda i: (i, 0)),
            pl.BlockSpec((4, 128), lambda i: (0, 0)),
        ],
        out_specs=[
            pl.BlockSpec((TILE, FEAT), lambda i: (i, 0)),
            pl.BlockSpec((ROWS // steps, FEAT), lambda i: (i, 0)),
            pl.BlockSpec((FEAT // steps, CODES), lambda i: (i, 0)),
            pl.BlockSpec((4, 128), lambda i: (0, 0)),
        ],
        out_shape=[
            jax.ShapeDtypeStruct((TABLE, FEAT), BF16),
            jax.ShapeDtypeStruct((ROWS, FEAT), BF16),
            jax.ShapeDtypeStruct((FEAT, CODES), BF16),
            jax.ShapeDtypeStruct((4, 128), F32),
        ],
        compiler_params=pltpu.CompilerParams(vmem_limit_bytes=60 * 1024 * 1024),
        name="grad_codes",
    )(returned, asked, grad_hidden, grad_sub, loss)
    return loss.reshape(ROWS), grad_hidden, grad_codes, grad_sub


def solution(mesh):
    return jax.shard_map(
        per_device,
        mesh=mesh,
        in_specs=(P("row", "col"), P("row", "col"), P("row"), P("row"), P("row", "col")),
        out_specs=(P("row"), P("row", "col"), P("row", "col"), P("row", "col")),
        check_vma=False,
    )
```

```python
import jax
import jax.numpy as jnp
from jax import lax
from jax.experimental import pallas as pl
from jax.experimental.pallas import tpu as pltpu
from jax.sharding import PartitionSpec as P

MESH = pl.DeviceIdType.MESH
F32, BF16, I32 = jnp.float32, jnp.bfloat16, jnp.int32

NX, NY, NZ = 4, 4, 8
NR, NC = NX * NY, 2 * NZ
ROWS, FEAT, CODES = 512, 256, 512
HALF = 256
TABLE = 8192
CAP = 64
CHUNK = 1024
TILE = 2048
NT = (((1,), (1,)), ((), ()))


class Ids:
    def __init__(self):
        self.at = {}
        for name in ("want", "serve0", "serve1", "stat", "ret0", "ret1"):
            for rel in range(16):
                self((name, rel))
        for half in range(2):
            for j in range(5):
                for part in range(4):
                    self(("w", half, j, part))
                    self(("x", half, j, part))
        for way in (1, -1):
            for s in range(4):
                for h in range(2):
                    self(("q", way, s + 1, h))
                    self(("z", way, s, h))
        for dz in range(NZ):
            self(("gs", dz))
            for h in range(2):
                self(("qs", dz, h))

    def __call__(self, name):
        return self.at.setdefault(name, len(self.at))


IDS = Ids()
N_IDS = len(IDS.at)


def dot(a, b, dims=(((1,), (0,)), ((), ()))):
    return lax.dot_general(a, b, dims, preferred_element_type=F32)


def main_kernel(
    hid, table, lab, tgt, wsub,
    loss_o, gh_o, gs_o, ret_o, ask_o,
    wf, qf, tb, tf, wbuf, askv, askr, asks, srv32, srv, fet, pm, mm, tw, lg, dl, dlt,
    stat_s, stat_r, gqo, gqs, sibr, zr, gt, xq, xl, ghb, outb,
    lsem, tsem, ssem, rsem,
):
    row = lax.axis_index("row")
    col = lax.axis_index("col")
    x, y = row // NY, row % NY
    z, k = col // 2, col % 2

    def rdev(r):
        return (r, col)

    def cdev(c):
        return (row, c)

    def xn(d):
        return rdev(((x + d + NX) % NX) * NY + y)

    def yn(d):
        return rdev(x * NY + (y + d + NY) % NY)

    def zn(d):
        return cdev(((z + d + NZ) % NZ) * 2 + k)

    sib = cdev(z * 2 + 1 - k)

    def slot(dx, dy):
        return ((x + dx) % NX) * NY + (y + dy) % NY

    def cp(i, src, dst, dev):
        return pltpu.make_async_remote_copy(
            src_ref=src, dst_ref=dst, send_sem=ssem.at[i], recv_sem=rsem.at[i],
            device_id=dev, device_id_type=MESH,
        )

    sent = []

    def send(name, src, dst, dev):
        c = cp(IDS(name), src, dst, dev)
        c.start()
        sent.append(c)

    def recv(name, dst):
        cp(IDS(name), dst, dst, sib).wait_recv()

    def each_send(name, count, copy):
        @pl.loop(1, count)
        def _(rel):
            src, dst, dev = copy(rel)
            cp(IDS((name, 0)) + rel, src, dst, dev).start()

    def each_recv(name, count, dst):
        @pl.loop(1, count)
        def _(rel):
            cp(IDS((name, 0)) + rel, dst(rel), dst(rel), sib).wait_recv()

    def each_sent(name, count, src):
        @pl.loop(1, count)
        def _(rel):
            cp(IDS((name, 0)) + rel, src, src, sib).wait_send()

    def row_at(rel):
        return (row + rel + NR) % NR

    def col_at(rel):
        return (col + rel + NC) % NC

    own_w = pltpu.make_async_copy(wsub, wf.at[row], lsem.at[0])
    own_w.start()

    def table_copy(i):
        return pltpu.make_async_copy(
            table.at[pl.ds(i * CHUNK, CHUNK), :], tb.at[i], tsem.at[i]
        )

    for i in range(TABLE // CHUNK):
        table_copy(i).start()

    barrier = pltpu.get_barrier_semaphore()

    @pl.loop(1, 16)
    def _(rel):
        pl.semaphore_signal(barrier, inc=1, device_id=rdev(row_at(rel)), device_id_type=MESH)
        pl.semaphore_signal(barrier, inc=1, device_id=cdev(col_at(rel)), device_id_type=MESH)

    lab_row = jnp.concatenate([lab[i:i + 1, :] for i in range(4)], axis=1)
    owner = lax.shift_right_logical(lab_row, 13)
    off = lab_row & (TABLE - 1)
    member = (owner == lax.broadcasted_iota(I32, (NR, ROWS), 0)).astype(F32)
    before = (
        lax.broadcasted_iota(I32, (ROWS, ROWS), 0) < lax.broadcasted_iota(I32, (ROWS, ROWS), 1)
    ).astype(F32).astype(BF16)
    rank = jnp.sum(member * dot(member.astype(BF16), before), axis=0, keepdims=True)
    rank = rank.astype(I32)
    at_rank = (rank == lax.broadcasted_iota(I32, (128, ROWS), 0)).astype(F32).astype(BF16)
    hi = lax.shift_right_logical(off, 7).astype(F32)
    lo = (off & 127).astype(F32)
    both = jnp.concatenate([member * hi, member * lo], axis=0).astype(BF16)
    spread = dot(both, at_rank, NT)
    wanted = (spread[:NR] * 128.0 + spread[NR:]).astype(I32)
    for g in range(NR):
        wbuf[g] = jnp.broadcast_to(wanted[g:g + 1, :], (8, 128))
    place = owner * CAP + rank

    pl.semaphore_wait(barrier, 30)
    each_send("want", NR, lambda rel: (wbuf.at[row_at(rel)], askv.at[row], rdev(row_at(rel))))
    own_w.wait()

    def whalf(s, half, a=0, n=128):
        return wf.at[s, pl.ds(half * 128 + a, n), :]

    def wring(half, j):
        if j == 4:
            return (xn, lambda d: slot(d, 0)) if half == 0 else (yn, lambda d: slot(0, d))
        if half == 0:
            return yn, lambda d: slot(j, d)
        return xn, lambda d: slot(d, j)

    def w_own(half, j):
        nb, at = wring(half, j)
        send(("w", half, j, 0), whalf(at(0), half), whalf(at(0), half), nb(1))
        send(("w", half, j, 1), whalf(at(0), half), whalf(at(0), half), nb(-1))

    def w_mid(half, j, side):
        nb, at = wring(half, j)
        s = at(3) if side == 0 else at(1)
        recv(("w", half, j, side), whalf(s, half))
        part = whalf(s, half, 64 * side, 64)
        send(("w", half, j, 2 + side), part, part, nb(1 - 2 * side))

    def w_last(half, j):
        nb, at = wring(half, j)
        for side in range(2):
            recv(("w", half, j, 2 + side), whalf(at(2), half, 64 * side, 64))

    for half in range(2):
        w_own(half, 4)
    for half in range(2):
        w_own(half, 0)

    for i in range(TABLE // CHUNK):
        table_copy(i).wait()

        @pl.loop(0, CHUNK // 128)
        def _(t, i=i):
            v = tb[i, pl.ds(t * 128, 128), :].astype(F32)
            for h in range(2):
                tf[h, pl.ds(i * CHUNK + t * 128, 128), :] = v[:, h * 128:(h + 1) * 128]

    askv[row] = wbuf[row]
    each_recv("want", NR, lambda rel: askv.at[row_at(-rel)])
    for r in range(NR):
        askr[r:r + 1, :] = askv[r, 0:1, :]
    to_smem = pltpu.make_async_copy(askr, asks, lsem.at[1])
    to_smem.start()
    to_smem.wait()

    def gather(r):
        @pl.loop(0, CAP // 16)
        def _(t):
            picks = [asks[r, t * 16 + u] & (TABLE - 1) for u in range(16)]
            rows = [(tf[0, pl.ds(i, 1), :], tf[1, pl.ds(i, 1), :]) for i in picks]
            for u in range(16):
                for h in range(2):
                    srv32[h, pl.ds(t * 16 + u, 1), :] = rows[u][h]

    def serve(h, rel):
        to = (row + rel) % NR
        cp(IDS((f"serve{h}", 0)) + rel, srv.at[h, to], fet.at[h, row], rdev(to)).start()

    @pl.loop(1, NR)
    def _(rel):
        to = (row + rel) % NR
        gather(to)
        for h in range(2):
            srv[h, to] = srv32[h].astype(BF16)
        serve(0, rel)

    @pl.loop(1, NR)
    def _(rel):
        serve(1, rel)

    gather(row)
    for h in range(2):
        fet[h, row] = srv32[h].astype(BF16)

    for half in range(2):
        for side in range(2):
            w_mid(half, 4, side)
            w_own(half, 3 - 2 * side)
    for half in range(2):
        for side in range(2):
            w_mid(half, 0, side)

    place_f = place.astype(F32)
    lane = lax.broadcasted_iota(I32, (128, 128), 1)
    for i in range(4):
        wide = jnp.broadcast_to(place_f[:, i * 128:(i + 1) * 128], (128, 128)).T.astype(I32)
        for t in range(8):
            pm[i * 128:(i + 1) * 128, t * 128:(t + 1) * 128] = (
                wide == lane + t * 128
            ).astype(F32).astype(BF16)

    def qpart(s, h):
        return qf.at[s, h]

    for h in range(2):
        each_recv(f"serve{h}", NR, lambda rel: fet.at[h, row_at(-rel)])
        code = dot(pm[...], fet[h].reshape(NR * CAP, 128))
        qf[col, h] = (hid[:, h * 128:(h + 1) * 128].astype(F32) + code).astype(BF16)
        send(("qs", 0, h), qpart(col, h), qpart(col, h), sib)
        for way in (1, -1):
            send(("q", way, 1, h), qpart(col, h), qpart(col, h), zn(way))

    def q_step(s, h):
        for way in (1, -1):
            if s == 4 and (way == 1) != (h == 0):
                continue
            at = ((z - way * s + NZ) % NZ) * 2 + k
            piece = qpart(at, h)
            recv(("q", way, s, h), piece)
            send(("qs", (-way * s) % NZ, h), piece, piece, sib)
            if s < 3 or (s == 3 and (way == 1) == (h == 0)):
                send(("q", way, s + 1, h), piece, piece, zn(way))

    def logits_of(n_ways, s):
        for dz in ([s, NZ - s] if 0 < s < 4 else [s]):
            for h in range(2):
                recv(("qs", dz, h), qpart(((z + dz) % NZ) * 2 + 1 - k, h))

        @pl.loop(0, 2 * n_ways)
        def _(t):
            dz = jnp.where(t % n_ways == 0, s, NZ - s)
            core = t // n_ways
            at = ((z + dz) % NZ) * 2 + core
            for h in range(2):
                rows = pl.ds(h * HALF, HALF)
                q = jnp.concatenate([qf[at, 0, rows, :], qf[at, 1, rows, :]], axis=1)
                lg[rows, :] += dot(q, wf[at])

    for half in range(2):
        w_last(half, 4)
        w_own(half, 2)
    for j in (3, 1):
        for half in range(2):
            for side in range(2):
                w_mid(half, j, side)
    for i in range(4):
        tw[i * 128:(i + 1) * 128, :] = (
            jnp.broadcast_to(tgt[i:i + 1, :].astype(F32), (128, 128)).T.astype(I32) - col * CODES
        )
    for t in range(8):
        mm[t * 128:(t + 1) * 128, :] = (
            place == lax.broadcasted_iota(I32, (128, ROWS), 0) + t * 128
        ).astype(F32).astype(BF16)
    lg[...] = jnp.zeros((ROWS, CODES), F32)
    for h in range(2):
        q_step(1, h)
    for half in range(2):
        for side in range(2):
            w_mid(half, 2, side)
    for h in range(2):
        q_step(2, h)
    for j in (0, 3, 1, 2):
        for half in range(2):
            w_last(half, j)
    logits_of(1, 0)
    q_step(3, 0)
    logits_of(2, 1)
    q_step(3, 1)
    logits_of(2, 2)
    for h in range(2):
        q_step(4, h)
    logits_of(2, 3)
    logits_of(1, 4)

    def hit_of(i, j):
        return tw[i * 128:(i + 1) * 128, :] == lane + j * 128

    for i in range(4):
        rows = slice(i * 128, (i + 1) * 128)
        v = lg[rows, :]
        peak = jnp.max(v, axis=1, keepdims=True)
        log_sum = peak + jnp.log(jnp.sum(jnp.exp(v - peak), axis=1, keepdims=True))
        hits = jnp.concatenate([hit_of(i, j) for j in range(4)], axis=1)
        target = jnp.sum(jnp.where(hits, v, 0.0), axis=1, keepdims=True)
        pair = jnp.where(lane == 0, log_sum, jnp.where(lane == 1, target, 0.0)).T
        stat_s[i:i + 1, :] = pair[0:1, :]
        stat_s[4 + i:5 + i, :] = pair[1:2, :]
    stat_r[col] = stat_s[...]
    each_send("stat", NC, lambda rel: (stat_s, stat_r.at[col], cdev(col_at(rel))))
    each_recv("stat", NC, lambda rel: stat_r.at[col_at(-rel)])
    logs = stat_r[:, 0:4, :]
    top = jnp.max(logs, axis=0)
    log_total = top + jnp.log(jnp.sum(jnp.exp(logs - top[None]), axis=0))
    loss_o[...] = log_total - jnp.sum(stat_r[:, 4:8, :], axis=0)
    for i in range(4):
        wide = jnp.broadcast_to(log_total[i:i + 1, :], (128, 128)).T
        for j in range(4):
            v = lg[i * 128:(i + 1) * 128, j * 128:(j + 1) * 128]
            d = jnp.exp(v - wide) - hit_of(i, j).astype(F32)
            dl[i * 128:(i + 1) * 128, j * 128:(j + 1) * 128] = d.astype(BF16)
            dlt[j * 128:(j + 1) * 128, i * 128:(i + 1) * 128] = d.T.astype(BF16)

    def sib_block(dz):
        v = dot(dl[...], wf[((z + dz) % NZ) * 2 + 1 - k], NT).astype(BF16)
        for h in range(2):
            gqs[dz, h] = v[:, h * 128:(h + 1) * 128]
        send(("gs", dz), gqs.at[dz], sibr.at[dz], sib)

    def own_block(dz):
        v = dot(dl[...], wf[((z + dz) % NZ) * 2 + k], NT).astype(BF16)
        for h in range(2):
            gqo[dz, h] = v[:, h * 128:(h + 1) * 128]

    def grad_block(dz):
        sib_block(dz)
        own_block(dz)

    def pair_up(dz):
        recv(("gs", dz), sibr.at[dz])
        gqo[dz] = (gqo[dz].astype(F32) + sibr[dz].astype(F32)).astype(BF16)

    def sub_block(dx, dy):
        s = slot(dx, dy)
        gt[s] = dot(dlt[...], jnp.concatenate([qf[s, 0], qf[s, 1]], axis=1)).astype(BF16)

    def zpart(dz, h):
        return gqo.at[dz % NZ, h]

    def zsend(way, d, h):
        send(("z", way, d, h), zpart(way * (d + 1), h), zr.at[(1 - way) // 2, d, h], zn(way))

    def zadd(way, d, h):
        got = zr.at[(1 - way) // 2, d, h]
        recv(("z", way, d, h), got)
        part = zpart(way * d, h)
        part[...] = (part[...].astype(F32) + got[...].astype(F32)).astype(BF16)

    def xring(half, j):
        if j == 4:
            return (xn, lambda d: slot(d, 0)) if half == 0 else (yn, lambda d: slot(0, d))
        if half == 0:
            return yn, lambda d: slot(j, d)
        return xn, lambda d: slot(d, j)

    def xpart(s, half, a=0, n=256):
        return gt.at[s, pl.ds(half * 256 + a, n), :]

    def x_start(half, j):
        nb, at = xring(half, j)
        for side in range(2):
            send(("x", half, j, side), xpart(at(2), half, 128 * side, 128), xq.at[half, j, side], nb(1 - 2 * side))

    def x_mid(half, j):
        nb, at = xring(half, j)
        for side in range(2):
            got = xq.at[half, j, side]
            recv(("x", half, j, side), got)
            s = at(1) if side == 0 else at(3)
            part = xpart(s, half, 128 * side, 128)
            part[...] = (part[...].astype(F32) + got[...].astype(F32)).astype(BF16)
            send(("x", half, j, 2 + side), xpart(s, half), xl.at[half, j, side], nb(1 - 2 * side))

    def x_end(half, j):
        nb, at = xring(half, j)
        for side in range(2):
            recv(("x", half, j, 2 + side), xl.at[half, j, side])
        part = xpart(at(0), half)
        part[...] = (
            part[...].astype(F32) + xl[half, j, 0].astype(F32) + xl[half, j, 1].astype(F32)
        ).astype(BF16)

    sib_block(4)
    sub_block(2, 2)
    for half in range(2):
        x_start(half, 2)
    own_block(4)
    sib_block(3)
    sib_block(5)
    pair_up(4)
    zsend(1, 3, 0)
    zsend(-1, 3, 1)
    own_block(3)
    own_block(5)
    pair_up(3)
    pair_up(5)
    zsend(1, 2, 1)
    zsend(-1, 2, 0)
    for d in (1, 3, 0):
        sub_block(2, d)
        sub_block(d, 2)
        for half in range(2):
            x_start(half, d)
    grad_block(2)
    grad_block(6)
    for half in range(2):
        x_mid(half, 2)
    pair_up(2)
    pair_up(6)
    for way, h in ((1, 0), (-1, 1)):
        zadd(way, 3, h)
        zsend(way, 2, h)
    sub_block(1, 1)
    sub_block(3, 1)
    sub_block(1, 3)
    sub_block(3, 3)
    sub_block(1, 0)
    sub_block(0, 1)
    sub_block(3, 0)
    sub_block(0, 3)
    sub_block(0, 0)
    for j in (1, 3):
        for half in range(2):
            x_mid(half, j)
    for way, h in ((1, 1), (-1, 0)):
        zadd(way, 2, h)
        zsend(way, 1, h)
    grad_block(1)
    grad_block(7)
    grad_block(0)
    for half in range(2):
        x_end(half, 2)
        x_start(half, 4)
    for half in range(2):
        x_mid(half, 0)
    pair_up(1)
    pair_up(7)
    for way, h in ((1, 0), (-1, 1)):
        zadd(way, 2, h)
        zsend(way, 1, h)
    for way, h in ((1, 1), (-1, 0)):
        zadd(way, 1, h)
        zsend(way, 0, h)
    for half in range(2):
        x_end(half, 1)
        x_end(half, 3)
    for half in range(2):
        x_mid(half, 4)
    for way, h in ((1, 0), (-1, 1)):
        zadd(way, 1, h)
        zsend(way, 0, h)
    pair_up(0)
    for half in range(2):
        x_end(half, 0)

    for h in range(2):
        for way in (1, -1):
            recv(("z", way, 0, h), zr.at[(1 - way) // 2, 0, h])
        total = gqo[0, h].astype(F32) + zr[0, 0, h].astype(F32) + zr[1, 0, h].astype(F32)
        ghb[h] = total.astype(BF16)
        gh_o[:, h * 128:(h + 1) * 128] = ghb[h]
        for t in range(4):
            moved = dot(mm[t * 256:(t + 1) * 256, :], ghb[h]).astype(BF16)
            for u in range(4):
                outb[h, 4 * t + u] = moved[u * CAP:(u + 1) * CAP]
        each_send(f"ret{h}", NR, lambda rel: (outb.at[h, row_at(rel)], ret_o.at[h, row], rdev(row_at(rel))))
        ret_o[h, row] = outb[h, row]
    for t in range(NR // 2):
        ask_o[t:t + 1, :] = jnp.concatenate(
            [askv[2 * t, 0:1, :CAP], askv[2 * t + 1, 0:1, :CAP]], axis=1
        )
    for half in range(2):
        x_end(half, 4)
    gs_o[...] = gt[row].astype(F32).T.astype(BF16)
    for h in range(2):
        each_recv(f"ret{h}", NR, lambda rel: ret_o.at[h, row_at(-rel)])

    for c in sent:
        c.wait_send()

    each_sent("want", NR, wbuf.at[0])
    each_sent("stat", NC, stat_s)
    for h in range(2):
        each_sent(f"serve{h}", NR, srv.at[h, 0])
        each_sent(f"ret{h}", NR, outb.at[h, 0])


def scatter_kernel(ret, ask, gh, gs, loss, codes_o, gh_o, gs_o, loss_o):
    base = pl.program_id(0) * TILE
    rows = jnp.concatenate([ret[h].reshape(NR * CAP, 128) for h in range(2)], axis=1)
    slots = lax.broadcasted_iota(I32, (TILE, 128), 0)
    hits = jnp.concatenate(
        [(ask[t:t + 1, :] - base == slots).astype(F32).astype(BF16) for t in range(8)], axis=1
    )
    codes_o[...] = dot(hits, rows).astype(BF16)
    gh_o[...] = gh[...]
    gs_o[...] = gs[...]
    loss_o[...] = loss[...]


def per_device(hidden_rows, code_table, labels, targets, sub_codebook):
    vmem = pl.BlockSpec(memory_space=pltpu.VMEM)
    loss, grad_hidden, grad_sub, returned, asked = pl.pallas_call(
        main_kernel,
        out_shape=(
            jax.ShapeDtypeStruct((4, 128), F32),
            jax.ShapeDtypeStruct((ROWS, FEAT), BF16),
            jax.ShapeDtypeStruct((FEAT, CODES), BF16),
            jax.ShapeDtypeStruct((2, NR, CAP, 128), BF16),
            jax.ShapeDtypeStruct((8, 128), I32),
        ),
        in_specs=[vmem, pl.BlockSpec(memory_space=pl.ANY), vmem, vmem, vmem],
        out_specs=[vmem] * 5,
        scratch_shapes=[
            pltpu.VMEM((NR, FEAT, CODES), BF16),
            pltpu.VMEM((NC, 2, ROWS, 128), BF16),
            pltpu.VMEM((TABLE // CHUNK, CHUNK, FEAT), BF16),
            pltpu.VMEM((2, TABLE, 128), F32),
            pltpu.VMEM((NR, 8, 128), I32),
            pltpu.VMEM((NR, 8, 128), I32),
            pltpu.VMEM((NR, 128), I32),
            pltpu.SMEM((NR, 128), I32),
            pltpu.VMEM((2, CAP, 128), F32),
            pltpu.VMEM((2, NR, CAP, 128), BF16),
            pltpu.VMEM((2, NR, CAP, 128), BF16),
            pltpu.VMEM((ROWS, NR * CAP), BF16),
            pltpu.VMEM((NR * CAP, ROWS), BF16),
            pltpu.VMEM((ROWS, 128), I32),
            pltpu.VMEM((ROWS, CODES), F32),
            pltpu.VMEM((ROWS, CODES), BF16),
            pltpu.VMEM((CODES, ROWS), BF16),
            pltpu.VMEM((8, 128), F32),
            pltpu.VMEM((NC, 8, 128), F32),
            pltpu.VMEM((NZ, 2, ROWS, 128), BF16),
            pltpu.VMEM((NZ, 2, ROWS, 128), BF16),
            pltpu.VMEM((NZ, 2, ROWS, 128), BF16),
            pltpu.VMEM((2, 4, 2, ROWS, 128), BF16),
            pltpu.VMEM((NR, CODES, FEAT), BF16),
            pltpu.VMEM((2, 5, 2, 128, FEAT), BF16),
            pltpu.VMEM((2, 5, 2, 256, FEAT), BF16),
            pltpu.VMEM((2, ROWS, 128), BF16),
            pltpu.VMEM((2, NR, CAP, 128), BF16),
            pltpu.SemaphoreType.DMA((2,)),
            pltpu.SemaphoreType.DMA((TABLE // CHUNK,)),
            pltpu.SemaphoreType.DMA((N_IDS,)),
            pltpu.SemaphoreType.DMA((N_IDS,)),
        ],
        compiler_params=pltpu.CompilerParams(
            collective_id=0, has_side_effects=True, vmem_limit_bytes=60 * 1024 * 1024
        ),
        name="exchange_and_gradients",
    )(hidden_rows, code_table, labels.reshape(4, 128), targets.reshape(4, 128), sub_codebook)
    steps = TABLE // TILE
    grad_codes, grad_hidden, grad_sub, loss = pl.pallas_call(
        scatter_kernel,
        grid=(steps,),
        in_specs=[
            pl.BlockSpec((2, NR, CAP, 128), lambda i: (0, 0, 0, 0)),
            pl.BlockSpec((8, 128), lambda i: (0, 0)),
            pl.BlockSpec((ROWS // steps, FEAT), lambda i: (i, 0)),
            pl.BlockSpec((FEAT // steps, CODES), lambda i: (i, 0)),
            pl.BlockSpec((4, 128), lambda i: (0, 0)),
        ],
        out_specs=[
            pl.BlockSpec((TILE, FEAT), lambda i: (i, 0)),
            pl.BlockSpec((ROWS // steps, FEAT), lambda i: (i, 0)),
            pl.BlockSpec((FEAT // steps, CODES), lambda i: (i, 0)),
            pl.BlockSpec((4, 128), lambda i: (0, 0)),
        ],
        out_shape=[
            jax.ShapeDtypeStruct((TABLE, FEAT), BF16),
            jax.ShapeDtypeStruct((ROWS, FEAT), BF16),
            jax.ShapeDtypeStruct((FEAT, CODES), BF16),
            jax.ShapeDtypeStruct((4, 128), F32),
        ],
        compiler_params=pltpu.CompilerParams(vmem_limit_bytes=60 * 1024 * 1024),
        name="grad_codes",
    )(returned, asked, grad_hidden, grad_sub, loss)
    return loss.reshape(ROWS), grad_hidden, grad_codes, grad_sub


def solution(mesh):
    return jax.shard_map(
        per_device,
        mesh=mesh,
        in_specs=(P("row", "col"), P("row", "col"), P("row"), P("row"), P("row", "col")),
        out_specs=(P("row"), P("row", "col"), P("row", "col"), P("row", "col")),
        check_vma=False,
    )
```

```python
import jax
import jax.numpy as jnp
from jax import lax
from jax.experimental import pallas as pl
from jax.experimental.pallas import tpu as pltpu
from jax.sharding import PartitionSpec as P

MESH = pl.DeviceIdType.MESH
F32, BF16, I32 = jnp.float32, jnp.bfloat16, jnp.int32

NX, NY, NZ = 4, 4, 8
NR, NC = NX * NY, 2 * NZ
ROWS, FEAT, CODES = 512, 256, 512
HALF = 256
TABLE = 8192
CAP = 64
CHUNK = 1024
TILE = 2048
NT = (((1,), (1,)), ((), ()))


class Ids:
    def __init__(self):
        self.at = {}
        for name in ("want", "serve0", "serve1", "stat", "ret0", "ret1"):
            for rel in range(16):
                self((name, rel))
        for half in range(2):
            for j in range(5):
                for part in range(4):
                    self(("w", half, j, part))
                    self(("x", half, j, part))
        for way in (1, -1):
            for s in range(4):
                for h in range(2):
                    self(("q", way, s + 1, h))
                    self(("z", way, s, h))
        for dz in range(NZ):
            self(("gs", dz))
            for h in range(2):
                self(("qs", dz, h))

    def __call__(self, name):
        return self.at.setdefault(name, len(self.at))


IDS = Ids()
N_IDS = len(IDS.at)


def dot(a, b, dims=(((1,), (0,)), ((), ()))):
    return lax.dot_general(a, b, dims, preferred_element_type=F32)


def main_kernel(
    hid_h, table, lab, tgt, wsub,
    loss_o, gh_h, gs_h, ret_h, ask_o,
    wf, qf, tb, tf, wbuf, askv, askr, asks, srv32, srv, fet, pm, mm, tw, lg, dl, dlt,
    stat_s, stat_r, gqo, gqs, sibr, zr, gt, xq, xl, ghb, outb,
    hid, gh_o, gs_o, ret_o, lsem, tsem, ssem, rsem,
):
    row = lax.axis_index("row")
    col = lax.axis_index("col")
    x, y = row // NY, row % NY
    z, k = col // 2, col % 2

    def rdev(r):
        return (r, col)

    def cdev(c):
        return (row, c)

    def xn(d):
        return rdev(((x + d + NX) % NX) * NY + y)

    def yn(d):
        return rdev(x * NY + (y + d + NY) % NY)

    def zn(d):
        return cdev(((z + d + NZ) % NZ) * 2 + k)

    sib = cdev(z * 2 + 1 - k)

    def slot(dx, dy):
        return ((x + dx) % NX) * NY + (y + dy) % NY

    def cp(i, src, dst, dev):
        return pltpu.make_async_remote_copy(
            src_ref=src, dst_ref=dst, send_sem=ssem.at[i], recv_sem=rsem.at[i],
            device_id=dev, device_id_type=MESH,
        )

    sent = []

    def send(name, src, dst, dev):
        c = cp(IDS(name), src, dst, dev)
        c.start()
        sent.append(c)

    def recv(name, dst):
        cp(IDS(name), dst, dst, sib).wait_recv()

    own_w = pltpu.make_async_copy(wsub, wf.at[row], lsem.at[0])
    own_w.start()
    hid_in = pltpu.make_async_copy(hid_h, hid, lsem.at[2])
    hid_in.start()
    gh_out = pltpu.make_async_copy(gh_o, gh_h, lsem.at[3])
    gs_out = pltpu.make_async_copy(gs_o, gs_h, lsem.at[4])

    def table_copy(i):
        return pltpu.make_async_copy(
            table.at[pl.ds(i * CHUNK, CHUNK), :], tb.at[i], tsem.at[i]
        )

    for i in range(TABLE // CHUNK):
        table_copy(i).start()

    barrier = pltpu.get_barrier_semaphore()
    for rel in range(1, 16):
        pl.semaphore_signal(barrier, inc=1, device_id=rdev((row + rel) % NR), device_id_type=MESH)
        pl.semaphore_signal(barrier, inc=1, device_id=cdev((col + rel) % NC), device_id_type=MESH)

    lab_row = jnp.concatenate([lab[i:i + 1, :] for i in range(4)], axis=1)
    owner = lax.shift_right_logical(lab_row, 13)
    off = lab_row & (TABLE - 1)
    member = (owner == lax.broadcasted_iota(I32, (NR, ROWS), 0)).astype(F32)
    before = (
        lax.broadcasted_iota(I32, (ROWS, ROWS), 0) < lax.broadcasted_iota(I32, (ROWS, ROWS), 1)
    ).astype(F32).astype(BF16)
    rank = jnp.sum(member * dot(member.astype(BF16), before), axis=0, keepdims=True)
    rank = rank.astype(I32)
    at_rank = (rank == lax.broadcasted_iota(I32, (128, ROWS), 0)).astype(F32).astype(BF16)
    hi = lax.shift_right_logical(off, 7).astype(F32)
    lo = (off & 127).astype(F32)
    both = jnp.concatenate([member * hi, member * lo], axis=0).astype(BF16)
    spread = dot(both, at_rank, NT)
    wanted = (spread[:NR] * 128.0 + spread[NR:]).astype(I32)
    for g in range(NR):
        wbuf[g] = jnp.broadcast_to(wanted[g:g + 1, :], (8, 128))
    place = owner * CAP + rank

    pl.semaphore_wait(barrier, 30)
    for rel in range(1, NR):
        to = (row + rel) % NR
        send(("want", rel), wbuf.at[to], askv.at[row], rdev(to))
    own_w.wait()

    def whalf(s, half, a=0, n=128):
        return wf.at[s, pl.ds(half * 128 + a, n), :]

    def wring(half, j):
        if j == 4:
            return (xn, lambda d: slot(d, 0)) if half == 0 else (yn, lambda d: slot(0, d))
        if half == 0:
            return yn, lambda d: slot(j, d)
        return xn, lambda d: slot(d, j)

    def w_own(half, j):
        nb, at = wring(half, j)
        send(("w", half, j, 0), whalf(at(0), half), whalf(at(0), half), nb(1))
        send(("w", half, j, 1), whalf(at(0), half), whalf(at(0), half), nb(-1))

    def w_mid(half, j, side):
        nb, at = wring(half, j)
        s = at(3) if side == 0 else at(1)
        recv(("w", half, j, side), whalf(s, half))
        part = whalf(s, half, 64 * side, 64)
        send(("w", half, j, 2 + side), part, part, nb(1 - 2 * side))

    def w_last(half, j):
        nb, at = wring(half, j)
        for side in range(2):
            recv(("w", half, j, 2 + side), whalf(at(2), half, 64 * side, 64))

    for half in range(2):
        w_own(half, 4)
    for half in range(2):
        w_own(half, 0)

    for i in range(TABLE // CHUNK):
        table_copy(i).wait()

        @pl.loop(0, CHUNK // 128)
        def _(t, i=i):
            v = tb[i, pl.ds(t * 128, 128), :].astype(F32)
            for h in range(2):
                tf[h, pl.ds(i * CHUNK + t * 128, 128), :] = v[:, h * 128:(h + 1) * 128]

    place_f = place.astype(F32)
    lane = lax.broadcasted_iota(I32, (128, 128), 1)
    for i in range(4):
        wide = jnp.broadcast_to(place_f[:, i * 128:(i + 1) * 128], (128, 128)).T.astype(I32)
        for t in range(8):
            pm[i * 128:(i + 1) * 128, t * 128:(t + 1) * 128] = (
                wide == lane + t * 128
            ).astype(F32).astype(BF16)

    askv[row] = wbuf[row]
    for rel in range(1, NR):
        recv(("want", rel), askv.at[(row - rel + NR) % NR])
    for r in range(NR):
        askr[r:r + 1, :] = askv[r, 0:1, :]
    to_smem = pltpu.make_async_copy(askr, asks, lsem.at[1])
    to_smem.start()
    to_smem.wait()

    def gather(r):
        @pl.loop(0, CAP // 16)
        def _(t):
            picks = [asks[r, t * 16 + u] & (TABLE - 1) for u in range(16)]
            rows = [(tf[0, pl.ds(i, 1), :], tf[1, pl.ds(i, 1), :]) for i in picks]
            for u in range(16):
                for h in range(2):
                    srv32[h, pl.ds(t * 16 + u, 1), :] = rows[u][h]

    def serve(h, rel):
        to = (row + rel) % NR
        cp(IDS((f"serve{h}", 0)) + rel, srv.at[h, to], fet.at[h, row], rdev(to)).start()

    @pl.loop(1, NR)
    def _(rel):
        to = (row + rel) % NR
        gather(to)
        for h in range(2):
            srv[h, to] = srv32[h].astype(BF16)
        serve(0, rel)

    @pl.loop(1, NR)
    def _(rel):
        serve(1, rel)

    gather(row)
    for h in range(2):
        fet[h, row] = srv32[h].astype(BF16)

    for half in range(2):
        for side in range(2):
            w_mid(half, 4, side)
            w_own(half, 3 - 2 * side)
    for half in range(2):
        for side in range(2):
            w_mid(half, 0, side)

    def qpart(s, h):
        return qf.at[s, h]

    hid_in.wait()

    for h in range(2):
        for rel in range(1, NR):
            recv((f"serve{h}", rel), fet.at[h, (row - rel + NR) % NR])
        code = dot(pm[...], fet[h].reshape(NR * CAP, 128))
        qf[col, h] = (hid[:, h * 128:(h + 1) * 128].astype(F32) + code).astype(BF16)
        send(("qs", 0, h), qpart(col, h), qpart(col, h), sib)
        for way in (1, -1):
            send(("q", way, 1, h), qpart(col, h), qpart(col, h), zn(way))

    def q_step(s, h):
        for way in (1, -1):
            if s == 4 and (way == 1) != (h == 0):
                continue
            at = ((z - way * s + NZ) % NZ) * 2 + k
            piece = qpart(at, h)
            recv(("q", way, s, h), piece)
            send(("qs", (-way * s) % NZ, h), piece, piece, sib)
            if s < 3 or (s == 3 and (way == 1) == (h == 0)):
                send(("q", way, s + 1, h), piece, piece, zn(way))

    def logits_of(n_ways, s):
        for dz in ([s, NZ - s] if 0 < s < 4 else [s]):
            for h in range(2):
                recv(("qs", dz, h), qpart(((z + dz) % NZ) * 2 + 1 - k, h))

        @pl.loop(0, 2 * n_ways)
        def _(t):
            dz = jnp.where(t % n_ways == 0, s, NZ - s)
            core = t // n_ways
            at = ((z + dz) % NZ) * 2 + core
            for h in range(2):
                rows = pl.ds(h * HALF, HALF)
                q = jnp.concatenate([qf[at, 0, rows, :], qf[at, 1, rows, :]], axis=1)
                lg[rows, :] += dot(q, wf[at])

    for half in range(2):
        w_last(half, 4)
        w_own(half, 2)
    for j in (3, 1):
        for half in range(2):
            for side in range(2):
                w_mid(half, j, side)
    for i in range(4):
        tw[i * 128:(i + 1) * 128, :] = (
            jnp.broadcast_to(tgt[i:i + 1, :].astype(F32), (128, 128)).T.astype(I32) - col * CODES
        )
    for t in range(8):
        mm[t * 128:(t + 1) * 128, :] = (
            place == lax.broadcasted_iota(I32, (128, ROWS), 0) + t * 128
        ).astype(F32).astype(BF16)
    lg[...] = jnp.zeros((ROWS, CODES), F32)
    for h in range(2):
        q_step(1, h)
    for half in range(2):
        for side in range(2):
            w_mid(half, 2, side)
    for h in range(2):
        q_step(2, h)
    for j in (0, 3, 1, 2):
        for half in range(2):
            w_last(half, j)
    logits_of(1, 0)
    q_step(3, 0)
    logits_of(2, 1)
    q_step(3, 1)
    logits_of(2, 2)
    for h in range(2):
        q_step(4, h)
    logits_of(2, 3)
    logits_of(1, 4)

    def hit_of(i, j):
        return tw[i * 128:(i + 1) * 128, :] == lane + j * 128

    for i in range(4):
        rows = slice(i * 128, (i + 1) * 128)
        v = lg[rows, :]
        peak = jnp.max(v, axis=1, keepdims=True)
        log_sum = peak + jnp.log(jnp.sum(jnp.exp(v - peak), axis=1, keepdims=True))
        hits = jnp.concatenate([hit_of(i, j) for j in range(4)], axis=1)
        target = jnp.sum(jnp.where(hits, v, 0.0), axis=1, keepdims=True)
        pair = jnp.where(lane == 0, log_sum, jnp.where(lane == 1, target, 0.0)).T
        stat_s[i:i + 1, :] = pair[0:1, :]
        stat_s[4 + i:5 + i, :] = pair[1:2, :]
    stat_r[col] = stat_s[...]
    for rel in range(1, NC):
        send(("stat", rel), stat_s, stat_r.at[col], cdev((col + rel) % NC))
    for rel in range(1, NC):
        recv(("stat", rel), stat_r.at[(col - rel + NC) % NC])
    logs = stat_r[:, 0:4, :]
    top = jnp.max(logs, axis=0)
    log_total = top + jnp.log(jnp.sum(jnp.exp(logs - top[None]), axis=0))
    loss_o[...] = log_total - jnp.sum(stat_r[:, 4:8, :], axis=0)
    for i in range(4):
        wide = jnp.broadcast_to(log_total[i:i + 1, :], (128, 128)).T
        for j in range(4):
            v = lg[i * 128:(i + 1) * 128, j * 128:(j + 1) * 128]
            d = jnp.exp(v - wide) - hit_of(i, j).astype(F32)
            dl[i * 128:(i + 1) * 128, j * 128:(j + 1) * 128] = d.astype(BF16)
            dlt[j * 128:(j + 1) * 128, i * 128:(i + 1) * 128] = d.T.astype(BF16)

    def sib_block(dz):
        v = dot(dl[...], wf[((z + dz) % NZ) * 2 + 1 - k], NT).astype(BF16)
        for h in range(2):
            gqs[dz, h] = v[:, h * 128:(h + 1) * 128]
        send(("gs", dz), gqs.at[dz], sibr.at[dz], sib)

    def own_block(dz):
        v = dot(dl[...], wf[((z + dz) % NZ) * 2 + k], NT).astype(BF16)
        for h in range(2):
            gqo[dz, h] = v[:, h * 128:(h + 1) * 128]

    def grad_block(dz):
        sib_block(dz)
        own_block(dz)

    def pair_up(dz):
        recv(("gs", dz), sibr.at[dz])
        gqo[dz] = (gqo[dz].astype(F32) + sibr[dz].astype(F32)).astype(BF16)

    def sub_block(dx, dy):
        s = slot(dx, dy)
        gt[s] = dot(dlt[...], jnp.concatenate([qf[s, 0], qf[s, 1]], axis=1)).astype(BF16)

    def zpart(dz, h):
        return gqo.at[dz % NZ, h]

    def zsend(way, d, h):
        send(("z", way, d, h), zpart(way * (d + 1), h), zr.at[(1 - way) // 2, d, h], zn(way))

    def zadd(way, d, h):
        got = zr.at[(1 - way) // 2, d, h]
        recv(("z", way, d, h), got)
        part = zpart(way * d, h)
        part[...] = (part[...].astype(F32) + got[...].astype(F32)).astype(BF16)

    def xring(half, j):
        if j == 4:
            return (xn, lambda d: slot(d, 0)) if half == 0 else (yn, lambda d: slot(0, d))
        if half == 0:
            return yn, lambda d: slot(j, d)
        return xn, lambda d: slot(d, j)

    def xpart(s, half, a=0, n=256):
        return gt.at[s, pl.ds(half * 256 + a, n), :]

    def x_start(half, j):
        nb, at = xring(half, j)
        for side in range(2):
            send(("x", half, j, side), xpart(at(2), half, 128 * side, 128), xq.at[half, j, side], nb(1 - 2 * side))

    def x_mid(half, j):
        nb, at = xring(half, j)
        for side in range(2):
            got = xq.at[half, j, side]
            recv(("x", half, j, side), got)
            s = at(1) if side == 0 else at(3)
            part = xpart(s, half, 128 * side, 128)
            part[...] = (part[...].astype(F32) + got[...].astype(F32)).astype(BF16)
            send(("x", half, j, 2 + side), xpart(s, half), xl.at[half, j, side], nb(1 - 2 * side))

    def x_end(half, j):
        nb, at = xring(half, j)
        for side in range(2):
            recv(("x", half, j, 2 + side), xl.at[half, j, side])
        part = xpart(at(0), half)
        part[...] = (
            part[...].astype(F32) + xl[half, j, 0].astype(F32) + xl[half, j, 1].astype(F32)
        ).astype(BF16)

    sib_block(4)
    sub_block(2, 2)
    for half in range(2):
        x_start(half, 2)
    own_block(4)
    sib_block(3)
    sib_block(5)
    pair_up(4)
    zsend(1, 3, 0)
    zsend(-1, 3, 1)
    own_block(3)
    own_block(5)
    pair_up(3)
    pair_up(5)
    zsend(1, 2, 1)
    zsend(-1, 2, 0)
    for d in (1, 3, 0):
        sub_block(2, d)
        sub_block(d, 2)
        for half in range(2):
            x_start(half, d)
    grad_block(2)
    grad_block(6)
    for half in range(2):
        x_mid(half, 2)
    pair_up(2)
    pair_up(6)
    for way, h in ((1, 0), (-1, 1)):
        zadd(way, 3, h)
        zsend(way, 2, h)
    sub_block(1, 1)
    sub_block(3, 1)
    sub_block(1, 3)
    sub_block(3, 3)
    sub_block(1, 0)
    sub_block(0, 1)
    sub_block(3, 0)
    sub_block(0, 3)
    sub_block(0, 0)
    for j in (1, 3):
        for half in range(2):
            x_mid(half, j)
    for way, h in ((1, 1), (-1, 0)):
        zadd(way, 2, h)
        zsend(way, 1, h)
    grad_block(1)
    grad_block(7)
    grad_block(0)
    for half in range(2):
        x_end(half, 2)
        x_start(half, 4)
    for half in range(2):
        x_mid(half, 0)
    pair_up(1)
    pair_up(7)
    for way, h in ((1, 0), (-1, 1)):
        zadd(way, 2, h)
        zsend(way, 1, h)
    for way, h in ((1, 1), (-1, 0)):
        zadd(way, 1, h)
        zsend(way, 0, h)
    for half in range(2):
        x_end(half, 1)
        x_end(half, 3)
    for half in range(2):
        x_mid(half, 4)
    for way, h in ((1, 0), (-1, 1)):
        zadd(way, 1, h)
        zsend(way, 0, h)
    pair_up(0)
    for half in range(2):
        x_end(half, 0)

    for h in range(2):
        for way in (1, -1):
            recv(("z", way, 0, h), zr.at[(1 - way) // 2, 0, h])
        total = gqo[0, h].astype(F32) + zr[0, 0, h].astype(F32) + zr[1, 0, h].astype(F32)
        ghb[h] = total.astype(BF16)
        gh_o[:, h * 128:(h + 1) * 128] = ghb[h]
        for t in range(4):
            moved = dot(mm[t * 256:(t + 1) * 256, :], ghb[h]).astype(BF16)
            for u in range(4):
                outb[h, 4 * t + u] = moved[u * CAP:(u + 1) * CAP]
        for rel in range(1, NR):
            to = (row + rel) % NR
            send((f"ret{h}", rel), outb.at[h, to], ret_o.at[h, row], rdev(to))
        ret_o[h, row] = outb[h, row]
    gh_out.start()
    for t in range(NR // 2):
        ask_o[t:t + 1, :] = jnp.concatenate(
            [askv[2 * t, 0:1, :CAP], askv[2 * t + 1, 0:1, :CAP]], axis=1
        )
    for half in range(2):
        x_end(half, 4)
    gs_o[...] = gt[row].astype(F32).T.astype(BF16)
    gs_out.start()
    for h in range(2):
        for rel in range(1, NR):
            recv((f"ret{h}", rel), ret_o.at[h, (row - rel + NR) % NR])
        pltpu.make_async_copy(ret_o.at[h], ret_h.at[h], lsem.at[5 + h]).start()

    for c in sent:
        c.wait_send()

    for h in range(2):
        @pl.loop(1, NR)
        def _(rel, h=h):
            cp(IDS((f"serve{h}", 0)) + rel, srv.at[h, 0], fet.at[h, 0], sib).wait_send()

    gh_out.wait()
    gs_out.wait()
    for h in range(2):
        pltpu.make_async_copy(ret_o.at[h], ret_h.at[h], lsem.at[5 + h]).wait()


def scatter_kernel(ret, ask, gh, gs, loss, codes_o, gh_o, gs_o, loss_o):
    base = pl.program_id(0) * TILE
    rows = jnp.concatenate([ret[h].reshape(NR * CAP, 128) for h in range(2)], axis=1)
    slots = lax.broadcasted_iota(I32, (TILE, 128), 0)
    hits = jnp.concatenate(
        [(ask[t:t + 1, :] - base == slots).astype(F32).astype(BF16) for t in range(8)], axis=1
    )
    codes_o[...] = dot(hits, rows).astype(BF16)
    gh_o[...] = gh[...]
    gs_o[...] = gs[...]
    loss_o[...] = loss[...]


def per_device(hidden_rows, code_table, labels, targets, sub_codebook):
    vmem = pl.BlockSpec(memory_space=pltpu.VMEM)
    hbm = pl.BlockSpec(memory_space=pl.ANY)
    loss, grad_hidden, grad_sub, returned, asked = pl.pallas_call(
        main_kernel,
        out_shape=(
            jax.ShapeDtypeStruct((4, 128), F32),
            jax.ShapeDtypeStruct((ROWS, FEAT), BF16),
            jax.ShapeDtypeStruct((FEAT, CODES), BF16),
            jax.ShapeDtypeStruct((2, NR, CAP, 128), BF16),
            jax.ShapeDtypeStruct((8, 128), I32),
        ),
        in_specs=[hbm, hbm, vmem, vmem, hbm],
        out_specs=[vmem, hbm, hbm, hbm, vmem],
        scratch_shapes=[
            pltpu.VMEM((NR, FEAT, CODES), BF16),
            pltpu.VMEM((NC, 2, ROWS, 128), BF16),
            pltpu.VMEM((TABLE // CHUNK, CHUNK, FEAT), BF16),
            pltpu.VMEM((2, TABLE, 128), F32),
            pltpu.VMEM((NR, 8, 128), I32),
            pltpu.VMEM((NR, 8, 128), I32),
            pltpu.VMEM((NR, 128), I32),
            pltpu.SMEM((NR, 128), I32),
            pltpu.VMEM((2, CAP, 128), F32),
            pltpu.VMEM((2, NR, CAP, 128), BF16),
            pltpu.VMEM((2, NR, CAP, 128), BF16),
            pltpu.VMEM((ROWS, NR * CAP), BF16),
            pltpu.VMEM((NR * CAP, ROWS), BF16),
            pltpu.VMEM((ROWS, 128), I32),
            pltpu.VMEM((ROWS, CODES), F32),
            pltpu.VMEM((ROWS, CODES), BF16),
            pltpu.VMEM((CODES, ROWS), BF16),
            pltpu.VMEM((8, 128), F32),
            pltpu.VMEM((NC, 8, 128), F32),
            pltpu.VMEM((NZ, 2, ROWS, 128), BF16),
            pltpu.VMEM((NZ, 2, ROWS, 128), BF16),
            pltpu.VMEM((NZ, 2, ROWS, 128), BF16),
            pltpu.VMEM((2, 4, 2, ROWS, 128), BF16),
            pltpu.VMEM((NR, CODES, FEAT), BF16),
            pltpu.VMEM((2, 5, 2, 128, FEAT), BF16),
            pltpu.VMEM((2, 5, 2, 256, FEAT), BF16),
            pltpu.VMEM((2, ROWS, 128), BF16),
            pltpu.VMEM((2, NR, CAP, 128), BF16),
            pltpu.VMEM((ROWS, FEAT), BF16),
            pltpu.VMEM((ROWS, FEAT), BF16),
            pltpu.VMEM((FEAT, CODES), BF16),
            pltpu.VMEM((2, NR, CAP, 128), BF16),
            pltpu.SemaphoreType.DMA((7,)),
            pltpu.SemaphoreType.DMA((TABLE // CHUNK,)),
            pltpu.SemaphoreType.DMA((N_IDS,)),
            pltpu.SemaphoreType.DMA((N_IDS,)),
        ],
        compiler_params=pltpu.CompilerParams(
            collective_id=0, has_side_effects=True, vmem_limit_bytes=60 * 1024 * 1024
        ),
        name="exchange_and_gradients",
    )(hidden_rows, code_table, labels.reshape(4, 128), targets.reshape(4, 128), sub_codebook)
    steps = TABLE // TILE
    grad_codes, grad_hidden, grad_sub, loss = pl.pallas_call(
        scatter_kernel,
        grid=(steps,),
        in_specs=[
            pl.BlockSpec((2, NR, CAP, 128), lambda i: (0, 0, 0, 0)),
            pl.BlockSpec((8, 128), lambda i: (0, 0)),
            pl.BlockSpec((ROWS // steps, FEAT), lambda i: (i, 0)),
            pl.BlockSpec((FEAT // steps, CODES), lambda i: (i, 0)),
            pl.BlockSpec((4, 128), lambda i: (0, 0)),
        ],
        out_specs=[
            pl.BlockSpec((TILE, FEAT), lambda i: (i, 0)),
            pl.BlockSpec((ROWS // steps, FEAT), lambda i: (i, 0)),
            pl.BlockSpec((FEAT // steps, CODES), lambda i: (i, 0)),
            pl.BlockSpec((4, 128), lambda i: (0, 0)),
        ],
        out_shape=[
            jax.ShapeDtypeStruct((TABLE, FEAT), BF16),
            jax.ShapeDtypeStruct((ROWS, FEAT), BF16),
            jax.ShapeDtypeStruct((FEAT, CODES), BF16),
            jax.ShapeDtypeStruct((4, 128), F32),
        ],
        compiler_params=pltpu.CompilerParams(vmem_limit_bytes=60 * 1024 * 1024),
        name="grad_codes",
    )(returned, asked, grad_hidden, grad_sub, loss)
    return loss.reshape(ROWS), grad_hidden, grad_codes, grad_sub


def solution(mesh):
    return jax.shard_map(
        per_device,
        mesh=mesh,
        in_specs=(P("row", "col"), P("row", "col"), P("row"), P("row"), P("row", "col")),
        out_specs=(P("row"), P("row", "col"), P("row", "col"), P("row", "col")),
        check_vma=False,
    )
```

```python
import jax
import jax.numpy as jnp
from jax import lax
from jax.experimental import pallas as pl
from jax.experimental.pallas import tpu as pltpu
from jax.sharding import PartitionSpec as P

MESH = pl.DeviceIdType.MESH
F32, BF16, I32 = jnp.float32, jnp.bfloat16, jnp.int32

NX, NY, NZ = 4, 4, 8
NR, NC = NX * NY, 2 * NZ
ROWS, FEAT, CODES = 512, 256, 512
HALF = 256
TABLE = 8192
CAP = 64
CHUNK = 1024
TILE = 2048
NT = (((1,), (1,)), ((), ()))


class Ids:
    def __init__(self):
        self.at = {}
        for name in ("want", "serve0", "serve1", "stat", "ret0", "ret1"):
            for rel in range(16):
                self((name, rel))
        for half in range(2):
            for j in range(5):
                for part in range(4):
                    self(("w", half, j, part))
                    self(("x", half, j, part))
        for way in (1, -1):
            for s in range(4):
                for h in range(2):
                    self(("q", way, s + 1, h))
                    self(("z", way, s, h))
        for dz in range(NZ):
            self(("gs", dz))
            for h in range(2):
                self(("qs", dz, h))

    def __call__(self, name):
        return self.at.setdefault(name, len(self.at))


IDS = Ids()
N_IDS = len(IDS.at)


def dot(a, b, dims=(((1,), (0,)), ((), ()))):
    return lax.dot_general(a, b, dims, preferred_element_type=F32)


def main_kernel(
    hid_h, table, lab, tgt, wsub,
    loss_o, gh_h, gs_h, ret_h, ask_o,
    wf, qf, tb, tf, wbuf, askv, askr, asks, srv32, srv, fet, pm, mm, tw, lg, dl, dlt,
    stat_s, stat_r, gqo, gqs, sibr, zr, gt, xq, xl, ghb, outb,
    hid, gh_o, gs_o, ret_o, lsem, tsem, ssem, rsem,
):
    row = lax.axis_index("row")
    col = lax.axis_index("col")
    x, y = row // NY, row % NY
    z, k = col // 2, col % 2

    def rdev(r):
        return (r, col)

    def cdev(c):
        return (row, c)

    def xn(d):
        return rdev(((x + d + NX) % NX) * NY + y)

    def yn(d):
        return rdev(x * NY + (y + d + NY) % NY)

    def zn(d):
        return cdev(((z + d + NZ) % NZ) * 2 + k)

    sib = cdev(z * 2 + 1 - k)

    def slot(dx, dy):
        return ((x + dx) % NX) * NY + (y + dy) % NY

    def cp(i, src, dst, dev):
        return pltpu.make_async_remote_copy(
            src_ref=src, dst_ref=dst, send_sem=ssem.at[i], recv_sem=rsem.at[i],
            device_id=dev, device_id_type=MESH,
        )

    sent = []

    def send(name, src, dst, dev):
        c = cp(IDS(name), src, dst, dev)
        c.start()
        sent.append(c)

    def recv(name, dst):
        cp(IDS(name), dst, dst, sib).wait_recv()

    own_w = pltpu.make_async_copy(wsub, wf.at[row], lsem.at[0])
    own_w.start()
    hid_in = pltpu.make_async_copy(hid_h, hid, lsem.at[2])
    hid_in.start()
    gh_out = pltpu.make_async_copy(gh_o, gh_h, lsem.at[3])
    gs_out = pltpu.make_async_copy(gs_o, gs_h, lsem.at[4])

    def table_copy(i):
        return pltpu.make_async_copy(
            table.at[pl.ds(i * CHUNK, CHUNK), :], tb.at[i], tsem.at[i]
        )

    for i in range(TABLE // CHUNK):
        table_copy(i).start()

    barrier = pltpu.get_barrier_semaphore()
    for rel in range(1, 16):
        pl.semaphore_signal(barrier, inc=1, device_id=rdev((row + rel) % NR), device_id_type=MESH)
        pl.semaphore_signal(barrier, inc=1, device_id=cdev((col + rel) % NC), device_id_type=MESH)

    lab_row = jnp.concatenate([lab[i:i + 1, :] for i in range(4)], axis=1)
    owner = lax.shift_right_logical(lab_row, 13)
    off = lab_row & (TABLE - 1)
    member = (owner == lax.broadcasted_iota(I32, (NR, ROWS), 0)).astype(F32)
    before = (
        lax.broadcasted_iota(I32, (ROWS, ROWS), 0) < lax.broadcasted_iota(I32, (ROWS, ROWS), 1)
    ).astype(F32).astype(BF16)
    rank = jnp.sum(member * dot(member.astype(BF16), before), axis=0, keepdims=True)
    rank = rank.astype(I32)
    at_rank = (rank == lax.broadcasted_iota(I32, (128, ROWS), 0)).astype(F32).astype(BF16)
    hi = lax.shift_right_logical(off, 7).astype(F32)
    lo = (off & 127).astype(F32)
    both = jnp.concatenate([member * hi, member * lo], axis=0).astype(BF16)
    spread = dot(both, at_rank, NT)
    wanted = (spread[:NR] * 128.0 + spread[NR:]).astype(I32)
    for g in range(NR):
        wbuf[g] = jnp.broadcast_to(wanted[g:g + 1, :], (8, 128))
    place = owner * CAP + rank

    pl.semaphore_wait(barrier, 30)
    for rel in range(1, NR):
        to = (row + rel) % NR
        send(("want", rel), wbuf.at[to], askv.at[row], rdev(to))
    own_w.wait()

    def whalf(s, half, a=0, n=128):
        return wf.at[s, pl.ds(half * 128 + a, n), :]

    def wring(half, j):
        if j == 4:
            return (xn, lambda d: slot(d, 0)) if half == 0 else (yn, lambda d: slot(0, d))
        if half == 0:
            return yn, lambda d: slot(j, d)
        return xn, lambda d: slot(d, j)

    def w_own(half, j):
        nb, at = wring(half, j)
        send(("w", half, j, 0), whalf(at(0), half), whalf(at(0), half), nb(1))
        send(("w", half, j, 1), whalf(at(0), half), whalf(at(0), half), nb(-1))

    def w_mid(half, j, side):
        nb, at = wring(half, j)
        s = at(3) if side == 0 else at(1)
        recv(("w", half, j, side), whalf(s, half))
        part = whalf(s, half, 64 * side, 64)
        send(("w", half, j, 2 + side), part, part, nb(1 - 2 * side))

    def w_last(half, j):
        nb, at = wring(half, j)
        for side in range(2):
            recv(("w", half, j, 2 + side), whalf(at(2), half, 64 * side, 64))

    for half in range(2):
        w_own(half, 4)
    for half in range(2):
        w_own(half, 0)

    for i in range(TABLE // CHUNK):
        table_copy(i).wait()

        @pl.loop(0, CHUNK // 128)
        def _(t, i=i):
            v = tb[i, pl.ds(t * 128, 128), :].astype(F32)
            for h in range(2):
                tf[h, pl.ds(i * CHUNK + t * 128, 128), :] = v[:, h * 128:(h + 1) * 128]

    place_f = place.astype(F32)
    lane = lax.broadcasted_iota(I32, (128, 128), 1)
    for i in range(4):
        wide = jnp.broadcast_to(place_f[:, i * 128:(i + 1) * 128], (128, 128)).T.astype(I32)
        for t in range(8):
            pm[i * 128:(i + 1) * 128, t * 128:(t + 1) * 128] = (
                wide == lane + t * 128
            ).astype(F32).astype(BF16)

    askv[row] = wbuf[row]
    for rel in range(1, NR):
        recv(("want", rel), askv.at[(row - rel + NR) % NR])
    for r in range(NR):
        askr[r:r + 1, :] = askv[r, 0:1, :]
    to_smem = pltpu.make_async_copy(askr, asks, lsem.at[1])
    to_smem.start()
    to_smem.wait()

    def gather(r):
        @pl.loop(0, CAP // 16)
        def _(t):
            picks = [asks[r, t * 16 + u] & (TABLE - 1) for u in range(16)]
            rows = [(tf[0, pl.ds(i, 1), :], tf[1, pl.ds(i, 1), :]) for i in picks]
            for u in range(16):
                for h in range(2):
                    srv32[h, pl.ds(t * 16 + u, 1), :] = rows[u][h]

    def serve(h, rel):
        to = (row + rel) % NR
        cp(IDS((f"serve{h}", 0)) + rel, srv.at[h, to], fet.at[h, row], rdev(to)).start()

    @pl.loop(1, NR)
    def _(rel):
        to = (row + rel) % NR
        gather(to)
        for h in range(2):
            srv[h, to] = srv32[h].astype(BF16)
        serve(0, rel)

    @pl.loop(1, NR)
    def _(rel):
        serve(1, rel)

    gather(row)
    for h in range(2):
        fet[h, row] = srv32[h].astype(BF16)

    for half in range(2):
        for side in range(2):
            w_mid(half, 4, side)
            w_own(half, 3 - 2 * side)
    for half in range(2):
        for side in range(2):
            w_mid(half, 0, side)

    def qpart(s, h):
        return qf.at[s, h]

    hid_in.wait()

    for h in range(2):
        for rel in range(1, NR):
            recv((f"serve{h}", rel), fet.at[h, (row - rel + NR) % NR])
        code = dot(pm[...], fet[h].reshape(NR * CAP, 128))
        qf[col, h] = (hid[:, h * 128:(h + 1) * 128].astype(F32) + code).astype(BF16)
        send(("qs", 0, h), qpart(col, h), qpart(col, h), sib)
        for way in (1, -1):
            send(("q", way, 1, h), qpart(col, h), qpart(col, h), zn(way))

    def q_step(s, h):
        for way in (1, -1):
            if s == 4 and (way == 1) != (h == 0):
                continue
            at = ((z - way * s + NZ) % NZ) * 2 + k
            piece = qpart(at, h)
            recv(("q", way, s, h), piece)
            send(("qs", (-way * s) % NZ, h), piece, piece, sib)
            if s < 3 or (s == 3 and (way == 1) == (h == 0)):
                send(("q", way, s + 1, h), piece, piece, zn(way))

    def logits_of(n_ways, s):
        for dz in ([s, NZ - s] if 0 < s < 4 else [s]):
            for h in range(2):
                recv(("qs", dz, h), qpart(((z + dz) % NZ) * 2 + 1 - k, h))

        @pl.loop(0, n_ways)
        def _(t):
            at = ((z + jnp.where(t == 0, s, NZ - s)) % NZ) * 2
            for h in range(2):
                rows = pl.ds(h * HALF, HALF)
                q = jnp.concatenate([qf[at + c, g, rows, :] for c in range(2) for g in range(2)], axis=1)
                lg[rows, :] += dot(q, wf[pl.ds(at, 2)].reshape(2 * FEAT, CODES))

    for half in range(2):
        w_last(half, 4)
        w_own(half, 2)
    for j in (3, 1):
        for half in range(2):
            for side in range(2):
                w_mid(half, j, side)
    for i in range(4):
        tw[i * 128:(i + 1) * 128, :] = (
            jnp.broadcast_to(tgt[i:i + 1, :].astype(F32), (128, 128)).T.astype(I32) - col * CODES
        )
    for t in range(8):
        mm[t * 128:(t + 1) * 128, :] = (
            place == lax.broadcasted_iota(I32, (128, ROWS), 0) + t * 128
        ).astype(F32).astype(BF16)
    lg[...] = jnp.zeros((ROWS, CODES), F32)
    for h in range(2):
        q_step(1, h)
    for half in range(2):
        for side in range(2):
            w_mid(half, 2, side)
    for h in range(2):
        q_step(2, h)
    for j in (0, 3, 1, 2):
        for half in range(2):
            w_last(half, j)
    logits_of(1, 0)
    q_step(3, 0)
    logits_of(2, 1)
    q_step(3, 1)
    logits_of(2, 2)
    logits_of(2, 3)
    for h in range(2):
        q_step(4, h)
    logits_of(1, 4)

    def hit_of(i, j):
        return tw[i * 128:(i + 1) * 128, :] == lane + j * 128

    for i in range(4):
        rows = slice(i * 128, (i + 1) * 128)
        v = lg[rows, :]
        peak = jnp.max(v, axis=1, keepdims=True)
        log_sum = peak + jnp.log(jnp.sum(jnp.exp(v - peak), axis=1, keepdims=True))
        hits = jnp.concatenate([hit_of(i, j) for j in range(4)], axis=1)
        target = jnp.sum(jnp.where(hits, v, 0.0), axis=1, keepdims=True)
        pair = jnp.where(lane == 0, log_sum, jnp.where(lane == 1, target, 0.0)).T
        stat_s[i:i + 1, :] = pair[0:1, :]
        stat_s[4 + i:5 + i, :] = pair[1:2, :]
    stat_r[col] = stat_s[...]
    for rel in range(1, NC):
        send(("stat", rel), stat_s, stat_r.at[col], cdev((col + rel) % NC))
    for rel in range(1, NC):
        recv(("stat", rel), stat_r.at[(col - rel + NC) % NC])
    logs = stat_r[:, 0:4, :]
    top = jnp.max(logs, axis=0)
    log_total = top + jnp.log(jnp.sum(jnp.exp(logs - top[None]), axis=0))
    loss_o[...] = log_total - jnp.sum(stat_r[:, 4:8, :], axis=0)
    for i in range(4):
        wide = jnp.broadcast_to(log_total[i:i + 1, :], (128, 128)).T
        for j in range(4):
            v = lg[i * 128:(i + 1) * 128, j * 128:(j + 1) * 128]
            d = jnp.exp(v - wide) - hit_of(i, j).astype(F32)
            dl[i * 128:(i + 1) * 128, j * 128:(j + 1) * 128] = d.astype(BF16)
            dlt[j * 128:(j + 1) * 128, i * 128:(i + 1) * 128] = d.T.astype(BF16)

    def sib_block(dz):
        v = dot(dl[...], wf[((z + dz) % NZ) * 2 + 1 - k], NT).astype(BF16)
        for h in range(2):
            gqs[dz, h] = v[:, h * 128:(h + 1) * 128]
        send(("gs", dz), gqs.at[dz], sibr.at[dz], sib)

    def own_block(dz):
        v = dot(dl[...], wf[((z + dz) % NZ) * 2 + k], NT).astype(BF16)
        for h in range(2):
            gqo[dz, h] = v[:, h * 128:(h + 1) * 128]

    def grad_block(dz):
        sib_block(dz)
        own_block(dz)

    def pair_up(dz):
        recv(("gs", dz), sibr.at[dz])
        gqo[dz] = (gqo[dz].astype(F32) + sibr[dz].astype(F32)).astype(BF16)

    def sub_block(dx, dy):
        s = slot(dx, dy)
        gt[s] = dot(dlt[...], jnp.concatenate([qf[s, 0], qf[s, 1]], axis=1)).astype(BF16)

    def zpart(dz, h):
        return gqo.at[dz % NZ, h]

    def zsend(way, d, h):
        send(("z", way, d, h), zpart(way * (d + 1), h), zr.at[(1 - way) // 2, d, h], zn(way))

    def zadd(way, d, h):
        got = zr.at[(1 - way) // 2, d, h]
        recv(("z", way, d, h), got)
        part = zpart(way * d, h)
        part[...] = (part[...].astype(F32) + got[...].astype(F32)).astype(BF16)

    def xring(half, j):
        if j == 4:
            return (xn, lambda d: slot(d, 0)) if half == 0 else (yn, lambda d: slot(0, d))
        if half == 0:
            return yn, lambda d: slot(j, d)
        return xn, lambda d: slot(d, j)

    def xpart(s, half, a=0, n=256):
        return gt.at[s, pl.ds(half * 256 + a, n), :]

    def x_start(half, j):
        nb, at = xring(half, j)
        for side in range(2):
            send(("x", half, j, side), xpart(at(2), half, 128 * side, 128), xq.at[half, j, side], nb(1 - 2 * side))

    def x_mid(half, j):
        nb, at = xring(half, j)
        for side in range(2):
            got = xq.at[half, j, side]
            recv(("x", half, j, side), got)
            s = at(1) if side == 0 else at(3)
            part = xpart(s, half, 128 * side, 128)
            part[...] = (part[...].astype(F32) + got[...].astype(F32)).astype(BF16)
            send(("x", half, j, 2 + side), xpart(s, half), xl.at[half, j, side], nb(1 - 2 * side))

    def x_end(half, j):
        nb, at = xring(half, j)
        for side in range(2):
            recv(("x", half, j, 2 + side), xl.at[half, j, side])
        part = xpart(at(0), half)
        part[...] = (
            part[...].astype(F32) + xl[half, j, 0].astype(F32) + xl[half, j, 1].astype(F32)
        ).astype(BF16)

    sib_block(4)
    sub_block(2, 2)
    for half in range(2):
        x_start(half, 2)
    own_block(4)
    sib_block(3)
    sib_block(5)
    pair_up(4)
    zsend(1, 3, 0)
    zsend(-1, 3, 1)
    own_block(3)
    own_block(5)
    pair_up(3)
    pair_up(5)
    zsend(1, 2, 1)
    zsend(-1, 2, 0)
    for d in (1, 3, 0):
        sub_block(2, d)
        sub_block(d, 2)
        for half in range(2):
            x_start(half, d)
    grad_block(2)
    grad_block(6)
    for half in range(2):
        x_mid(half, 2)
    pair_up(2)
    pair_up(6)
    for way, h in ((1, 0), (-1, 1)):
        zadd(way, 3, h)
        zsend(way, 2, h)
    sub_block(1, 1)
    sub_block(3, 1)
    sub_block(1, 3)
    sub_block(3, 3)
    sub_block(1, 0)
    sub_block(0, 1)
    sub_block(3, 0)
    sub_block(0, 3)
    sub_block(0, 0)
    for j in (1, 3):
        for half in range(2):
            x_mid(half, j)
    for way, h in ((1, 1), (-1, 0)):
        zadd(way, 2, h)
        zsend(way, 1, h)
    grad_block(1)
    grad_block(7)
    grad_block(0)
    for half in range(2):
        x_end(half, 2)
        x_start(half, 4)
    for half in range(2):
        x_mid(half, 0)
    pair_up(1)
    pair_up(7)
    for way, h in ((1, 0), (-1, 1)):
        zadd(way, 2, h)
        zsend(way, 1, h)
    for way, h in ((1, 1), (-1, 0)):
        zadd(way, 1, h)
        zsend(way, 0, h)
    for half in range(2):
        x_end(half, 1)
        x_end(half, 3)
    for half in range(2):
        x_mid(half, 4)
    for way, h in ((1, 0), (-1, 1)):
        zadd(way, 1, h)
        zsend(way, 0, h)
    pair_up(0)
    for half in range(2):
        x_end(half, 0)

    for h in range(2):
        for way in (1, -1):
            recv(("z", way, 0, h), zr.at[(1 - way) // 2, 0, h])
        total = gqo[0, h].astype(F32) + zr[0, 0, h].astype(F32) + zr[1, 0, h].astype(F32)
        ghb[h] = total.astype(BF16)
        gh_o[:, h * 128:(h + 1) * 128] = ghb[h]
        for t in range(4):
            moved = dot(mm[t * 256:(t + 1) * 256, :], ghb[h]).astype(BF16)
            for u in range(4):
                outb[h, 4 * t + u] = moved[u * CAP:(u + 1) * CAP]
        for rel in range(1, NR):
            to = (row + rel) % NR
            send((f"ret{h}", rel), outb.at[h, to], ret_o.at[h, row], rdev(to))
        ret_o[h, row] = outb[h, row]
    gh_out.start()
    for t in range(NR // 2):
        ask_o[t:t + 1, :] = jnp.concatenate(
            [askv[2 * t, 0:1, :CAP], askv[2 * t + 1, 0:1, :CAP]], axis=1
        )
    for half in range(2):
        x_end(half, 4)
    gs_o[...] = gt[row].astype(F32).T.astype(BF16)
    gs_out.start()
    for h in range(2):
        for rel in range(1, NR):
            recv((f"ret{h}", rel), ret_o.at[h, (row - rel + NR) % NR])
        pltpu.make_async_copy(ret_o.at[h], ret_h.at[h], lsem.at[5 + h]).start()

    for c in sent:
        c.wait_send()

    for h in range(2):
        @pl.loop(1, NR)
        def _(rel, h=h):
            cp(IDS((f"serve{h}", 0)) + rel, srv.at[h, 0], fet.at[h, 0], sib).wait_send()

    gh_out.wait()
    gs_out.wait()
    for h in range(2):
        pltpu.make_async_copy(ret_o.at[h], ret_h.at[h], lsem.at[5 + h]).wait()


def scatter_kernel(ret, ask, gh, gs, loss, codes_o, gh_o, gs_o, loss_o):
    base = pl.program_id(0) * TILE
    rows = jnp.concatenate([ret[h].reshape(NR * CAP, 128) for h in range(2)], axis=1)
    slots = lax.broadcasted_iota(I32, (TILE, 128), 0)
    hits = jnp.concatenate(
        [(ask[t:t + 1, :] - base == slots).astype(F32).astype(BF16) for t in range(8)], axis=1
    )
    codes_o[...] = dot(hits, rows).astype(BF16)
    gh_o[...] = gh[...]
    gs_o[...] = gs[...]
    loss_o[...] = loss[...]


def per_device(hidden_rows, code_table, labels, targets, sub_codebook):
    vmem = pl.BlockSpec(memory_space=pltpu.VMEM)
    hbm = pl.BlockSpec(memory_space=pl.ANY)
    loss, grad_hidden, grad_sub, returned, asked = pl.pallas_call(
        main_kernel,
        out_shape=(
            jax.ShapeDtypeStruct((4, 128), F32),
            jax.ShapeDtypeStruct((ROWS, FEAT), BF16),
            jax.ShapeDtypeStruct((FEAT, CODES), BF16),
            jax.ShapeDtypeStruct((2, NR, CAP, 128), BF16),
            jax.ShapeDtypeStruct((8, 128), I32),
        ),
        in_specs=[hbm, hbm, vmem, vmem, hbm],
        out_specs=[vmem, hbm, hbm, hbm, vmem],
        scratch_shapes=[
            pltpu.VMEM((NR, FEAT, CODES), BF16),
            pltpu.VMEM((NC, 2, ROWS, 128), BF16),
            pltpu.VMEM((TABLE // CHUNK, CHUNK, FEAT), BF16),
            pltpu.VMEM((2, TABLE, 128), F32),
            pltpu.VMEM((NR, 8, 128), I32),
            pltpu.VMEM((NR, 8, 128), I32),
            pltpu.VMEM((NR, 128), I32),
            pltpu.SMEM((NR, 128), I32),
            pltpu.VMEM((2, CAP, 128), F32),
            pltpu.VMEM((2, NR, CAP, 128), BF16),
            pltpu.VMEM((2, NR, CAP, 128), BF16),
            pltpu.VMEM((ROWS, NR * CAP), BF16),
            pltpu.VMEM((NR * CAP, ROWS), BF16),
            pltpu.VMEM((ROWS, 128), I32),
            pltpu.VMEM((ROWS, CODES), F32),
            pltpu.VMEM((ROWS, CODES), BF16),
            pltpu.VMEM((CODES, ROWS), BF16),
            pltpu.VMEM((8, 128), F32),
            pltpu.VMEM((NC, 8, 128), F32),
            pltpu.VMEM((NZ, 2, ROWS, 128), BF16),
            pltpu.VMEM((NZ, 2, ROWS, 128), BF16),
            pltpu.VMEM((NZ, 2, ROWS, 128), BF16),
            pltpu.VMEM((2, 4, 2, ROWS, 128), BF16),
            pltpu.VMEM((NR, CODES, FEAT), BF16),
            pltpu.VMEM((2, 5, 2, 128, FEAT), BF16),
            pltpu.VMEM((2, 5, 2, 256, FEAT), BF16),
            pltpu.VMEM((2, ROWS, 128), BF16),
            pltpu.VMEM((2, NR, CAP, 128), BF16),
            pltpu.VMEM((ROWS, FEAT), BF16),
            pltpu.VMEM((ROWS, FEAT), BF16),
            pltpu.VMEM((FEAT, CODES), BF16),
            pltpu.VMEM((2, NR, CAP, 128), BF16),
            pltpu.SemaphoreType.DMA((7,)),
            pltpu.SemaphoreType.DMA((TABLE // CHUNK,)),
            pltpu.SemaphoreType.DMA((N_IDS,)),
            pltpu.SemaphoreType.DMA((N_IDS,)),
        ],
        compiler_params=pltpu.CompilerParams(
            collective_id=0, has_side_effects=True, vmem_limit_bytes=60 * 1024 * 1024
        ),
        name="exchange_and_gradients",
    )(hidden_rows, code_table, labels.reshape(4, 128), targets.reshape(4, 128), sub_codebook)
    steps = TABLE // TILE
    grad_codes, grad_hidden, grad_sub, loss = pl.pallas_call(
        scatter_kernel,
        grid=(steps,),
        in_specs=[
            pl.BlockSpec((2, NR, CAP, 128), lambda i: (0, 0, 0, 0)),
            pl.BlockSpec((8, 128), lambda i: (0, 0)),
            pl.BlockSpec((ROWS // steps, FEAT), lambda i: (i, 0)),
            pl.BlockSpec((FEAT // steps, CODES), lambda i: (i, 0)),
            pl.BlockSpec((4, 128), lambda i: (0, 0)),
        ],
        out_specs=[
            pl.BlockSpec((TILE, FEAT), lambda i: (i, 0)),
            pl.BlockSpec((ROWS // steps, FEAT), lambda i: (i, 0)),
            pl.BlockSpec((FEAT // steps, CODES), lambda i: (i, 0)),
            pl.BlockSpec((4, 128), lambda i: (0, 0)),
        ],
        out_shape=[
            jax.ShapeDtypeStruct((TABLE, FEAT), BF16),
            jax.ShapeDtypeStruct((ROWS, FEAT), BF16),
            jax.ShapeDtypeStruct((FEAT, CODES), BF16),
            jax.ShapeDtypeStruct((4, 128), F32),
        ],
        compiler_params=pltpu.CompilerParams(vmem_limit_bytes=60 * 1024 * 1024),
        name="grad_codes",
    )(returned, asked, grad_hidden, grad_sub, loss)
    return loss.reshape(ROWS), grad_hidden, grad_codes, grad_sub


def solution(mesh):
    return jax.shard_map(
        per_device,
        mesh=mesh,
        in_specs=(P("row", "col"), P("row", "col"), P("row"), P("row"), P("row", "col")),
        out_specs=(P("row"), P("row", "col"), P("row", "col"), P("row", "col")),
        check_vma=False,
    )
```
